256 devices in a mesh: row: 16 (over y, z_lo, core), col: 16 (over x, z_hi).
Axes of the slice: x: 4, y: 4, z: 8 (z_hi: 4, z_lo: 2; z = z_hi * 2 + z_lo), core: 2. Of those that a mesh axis runs over, the one named last changes fastest.
Arguments:
- positions: float32 [4096, 147], P(('row', 'col')), may hold values from -0.55 to 9.45, as said below
- coefficients: float32 [4096, 147], P(('row', 'col')), may hold values from -6 to 6
- atom_pairs: int32 [2, 1176], replicated, may hold values from 0 to 48, as said below
- pair_scale: float32 [1176], replicated, may hold values from 0.5 to 2
Outputs:
- applied: float32 [4096, 147], P(('row', 'col'))
The draws below stay inside these ranges and needn't reach their ends.
Inputs may be any that keep to these rules, and one draw needn't show every extreme that they name: `atom_pairs`: every unordered pair of two different atoms stands in exactly one column, the smaller atom in row 0. `positions`: every two atoms of a geometry lie 0.6 or more apart; all geometries are displacements of one molecule.
All inputs are finite; a program needn't handle non-finite values.
Results may differ from the reference program's by a relative error of at most 0.0003.
Values sent between devices are 32-bit elements; how exact they have to be, the bound alone decides.
No kernel may reach another device: no remote copies, remote signals or barrier semaphores. Data moves between devices by JAX's collectives and lax.ppermute only.
A program may use at most 64 MiB of HBM per device.

```python
import math
import jax
import jax.numpy as jnp
import numpy as np
from jax import lax

ATOMS = 49
FEATURES = 1176
GEOMS = 4096


def draw_positions(key, part):
    base_key = jax.random.fold_in(key, 11)
    move_key = jax.random.fold_in(key, 12)
    lift_key = jax.random.fold_in(key, 13)
    atom_ids = jnp.arange(ATOMS, dtype=jnp.int32)
    grid = jnp.stack([(atom_ids % 7).astype(jnp.float32) * 1.5, (atom_ids // 7).astype(jnp.float32) * 1.5, jnp.zeros((ATOMS,), jnp.float32)], 0)
    jitter = jax.random.uniform(base_key, (3, ATOMS), jnp.float32, -1.0, 1.0) * jnp.array([0.2, 0.2, 0.3], jnp.float32)[:, None]
    planar = jax.random.uniform(move_key, (GEOMS, 2, ATOMS), jnp.float32, -0.25, 0.25)
    lifted = jax.random.uniform(lift_key, (GEOMS, 1, ATOMS), jnp.float32, -0.25, 3.0)
    moves = jnp.concatenate([planar, lifted], axis=1)
    return ((grid + jitter)[None] + moves).reshape(GEOMS, 3 * ATOMS)


def draw_atom_pairs(key, part):
    first, second = np.triu_indices(ATOMS, 1)
    table = jnp.asarray(np.stack([first, second]).astype(np.int32))
    order = jax.random.permutation(jax.random.fold_in(key, 21), FEATURES)
    return table[:, order]


def level_of(key, extent, cuts, smallest, largest):
    def one(dim, shards_of):
        heights = jax.random.uniform(jax.random.fold_in(jax.random.fold_in(key, 6), dim), (shards_of,), jnp.float32, smallest / len(cuts), largest / len(cuts))
        return jnp.repeat(jnp.exp(heights), extent[dim] // shards_of).reshape((-1,) + (1,) * (len(extent) - dim - 1))

    factor_of = one(*cuts[0])
    for cut in cuts[1:]:
        factor_of = factor_of * one(*cut)
    return factor_of


def gaussian(key, shape, deviation, bound, cuts=(), kind=jnp.bfloat16):
    factor_of = level_of(key, shape, cuts, -0.22, 0.18) if cuts else 1.0
    values = jax.random.normal(key, shape, jnp.float32) * deviation * factor_of
    return jnp.minimum(jnp.maximum(values, -bound), bound).astype(kind)


def setup_inputs(seed: int = 0) -> dict:
    arg_keys = jax.random.split(jax.random.key(seed), 5)
    return {
        "positions": draw_positions(jax.random.fold_in(arg_keys[4], 71), 0),
        "coefficients": gaussian(arg_keys[1], (GEOMS, 3 * ATOMS), 1.0, 6.0, ((0, 256),), jnp.float32),
        "atom_pairs": draw_atom_pairs(jax.random.fold_in(arg_keys[4], 71), 0),
        "pair_scale": jnp.clip(jnp.exp(jax.random.uniform(arg_keys[3], (FEATURES,), jnp.float32, math.log(0.5), math.log(2.0))), 0.5, 2.0),
    }


highest = lax.Precision.HIGHEST
length_scale = 2.0
decay_rate = math.sqrt(5.0) / length_scale
outer_factor = decay_rate * decay_rate / 3.0
radial_factor = decay_rate * decay_rate

def pair_table(atom_pairs, atoms):
    atom_ids = jnp.arange(atoms, dtype=jnp.int32)[:, None]
    first = (atom_ids == atom_pairs[0][None, :]).astype(jnp.float32)
    second = (atom_ids == atom_pairs[1][None, :]).astype(jnp.float32)
    return first - second

def geometry_terms(positions, coefficients, onehot, pair_scale):
    count = positions.shape[0]
    atoms = onehot.shape[0]
    spans = jnp.dot(positions.reshape(count * 3, atoms), onehot, precision=highest).reshape(count, 3, -1)
    moves = jnp.dot(coefficients.reshape(count * 3, atoms), onehot, precision=highest).reshape(count, 3, -1)
    inverse = 1.0 / jnp.sqrt(lax.optimization_barrier(jnp.sum(spans * spans, axis=1)))
    features = pair_scale[None, :] * inverse
    weights = features * inverse * inverse
    tangents = -weights * lax.optimization_barrier(jnp.sum(spans * moves, axis=1))
    return (features, tangents, spans, weights)

def pull_back(grads, spans, weights, onehot):
    count = grads.shape[0]
    terms = -(weights * grads)[:, None, :] * spans
    return jnp.dot(terms.reshape(count * 3, -1), onehot.T, precision=highest).reshape(count, -1)

def kernel_terms(rows_x, cols_x):
    gram = jnp.dot(rows_x, cols_x.T, precision=highest)
    sq_dist = lax.optimization_barrier(jnp.sum(rows_x * rows_x, axis=1))[:, None] + lax.optimization_barrier(jnp.sum(cols_x * cols_x, axis=1))[None, :] - 2.0 * gram
    radius = jnp.sqrt(jnp.maximum(sq_dist, 0.0))
    envelope = outer_factor * jnp.exp(-decay_rate * radius)
    return (envelope, envelope * (1.0 + decay_rate * radius))

def row_apply(rows_x, rows_u, cols_x, cols_u):
    envelope, direct = kernel_terms(rows_x, cols_x)
    cross = jnp.dot(rows_x, cols_u.T, precision=highest) - lax.optimization_barrier(jnp.sum(cols_x * cols_u, axis=1))[None, :]
    bent = envelope * cross
    return jnp.dot(direct, cols_u, precision=highest) - radial_factor * (lax.optimization_barrier(jnp.sum(bent, axis=1))[:, None] * rows_x - jnp.dot(bent, cols_x, precision=highest))

def reference(positions, coefficients, atom_pairs, pair_scale):
    total = positions.shape[0]
    atoms = positions.shape[1] // 3
    onehot = pair_table(atom_pairs, atoms)
    features, tangents, spans, weights = geometry_terms(positions, coefficients, onehot, pair_scale)
    block = math.gcd(total, 512)
    width = features.shape[1]

    def one_block(pieces):
        return row_apply(pieces[0], pieces[1], features, tangents)
    grads = lax.map(one_block, (features.reshape(total // block, block, width), tangents.reshape(total // block, block, width)))
    return pull_back(grads.reshape(total, width), spans, weights, onehot)
```

```python
import math

import jax
import jax.numpy as jnp
from jax import lax
from jax.experimental import pallas as pl
from jax.experimental.pallas import tpu as pltpu
from jax.sharding import PartitionSpec as P

ATOMS = 49
HALF = 24
BLOCK = 56
ROWS = HALF * BLOCK
WRAP = 80
CART = 3 * ATOMS
LANES = 128

length_scale = 2.0
decay_rate = math.sqrt(5.0) / length_scale
outer_factor = decay_rate * decay_rate / 3.0
radial_factor = decay_rate * decay_rate
f32 = jnp.float32
bf16 = jnp.bfloat16


def halves(value):
    high = value.astype(bf16)
    return high, (value - high.astype(f32)).astype(bf16)


def dot_nt(a, b):
    return lax.dot_general(a, b, (((1,), (1,)), ((), ())), preferred_element_type=f32)


def dot_nn(a, b):
    return lax.dot_general(a, b, (((1,), (0,)), ((), ())), preferred_element_type=f32)


def pack_kernel(p_ref, c_ref, rows_ref, cols_ref):
    half = p_ref.shape[0] // 2
    p, c = p_ref[...], c_ref[...]
    for n in range(rows_ref.shape[0]):
        rows_ref[n, :, 0:CART] = p[:half]
        rows_ref[n, :, CART : 2 * CART] = p[half:]
    for n in range(cols_ref.shape[0]):
        cols_ref[n, :, 0:CART] = p[:half]
        cols_ref[n, :, CART : 2 * CART] = p[half:]
        cols_ref[n, :, 2 * CART : 3 * CART] = c[:half]
        cols_ref[n, :, 3 * CART : 4 * CART] = c[half:]


def scale_kernel(pairs_ref, scale_ref, out_ref):
    low, high = pairs_ref[0:1, :], pairs_ref[1:2, :]
    apart = high - low
    near = apart <= HALF
    shift = jnp.where(near, apart, ATOMS - apart) - 1
    start = jnp.where(near, low, high)
    count = low.shape[1]
    atom_ids = lax.broadcasted_iota(jnp.int32, (64, count), 0)
    shift_ids = lax.broadcasted_iota(jnp.int32, (32, count), 0)
    at_atom = jnp.where(atom_ids == start, 1.0, 0.0).astype(bf16)
    scaled = jnp.where(shift_ids == shift, scale_ref[...], 0.0)
    top = scaled.astype(bf16)
    rest = scaled - top.astype(f32)
    middle = rest.astype(bf16)
    bottom = (rest - middle.astype(f32)).astype(bf16)
    table = dot_nt(at_atom, top) + dot_nt(at_atom, middle) + dot_nt(at_atom, bottom)
    for d in range(HALF):
        out_ref[d * BLOCK : (d + 1) * BLOCK, :] = jnp.broadcast_to(
            table[0:BLOCK, d : d + 1], (BLOCK, LANES)
        )


def wrap_rows(flat_ref, start, wrapped_ref, *at):
    for k in range(3):
        base = start + k * ATOMS
        wrapped_ref[(*at, k, slice(0, ATOMS), slice(None))] = flat_ref[base : base + ATOMS, :]
        wrapped_ref[(*at, k, slice(ATOMS, WRAP), slice(None))] = flat_ref[
            base : base + WRAP - ATOMS, :
        ]


def spans_of(wrapped_ref, at, d):
    return [
        wrapped_ref[(*at, k, slice(0, BLOCK), slice(None))]
        - wrapped_ref[(*at, k, slice(d, d + BLOCK), slice(None))]
        for k in range(3)
    ]


def fold8(value):
    total = value[0:8]
    for n in range(1, value.shape[0] // 8):
        total = total + value[8 * n : 8 * n + 8]
    return total


def apply_kernel(
    rows_ref, cols_ref, scale_ref, out_ref,
    flat_rows, flat_cols, rows_w, cols_p, cols_c, pair_hi, pair_lo, row_x, row_weight,
    rowx_hi, rowx_lo, grads, back, flat_out,
):
    flat_cols[...] = cols_ref[...].T
    flat_rows[...] = rows_ref[...].T
    for t in range(2):
        wrap_rows(flat_cols, t * CART, cols_p, t)
        wrap_rows(flat_cols, (2 + t) * CART, cols_c, t)
        wrap_rows(flat_rows, t * CART, rows_w, t)

    pad_one = (lax.broadcasted_iota(jnp.int32, (2 * BLOCK, LANES), 0) == ATOMS).astype(f32)
    col_sq, col_xu = [], []
    for t in range(2):
        sq, xu = jnp.zeros((8, LANES), f32), jnp.zeros((8, LANES), f32)
        lanes_x = slice(t * LANES, (t + 1) * LANES)
        lanes_u = slice((2 + t) * LANES, (3 + t) * LANES)
        for pair in range(HALF // 2):
            xs, us = [], []
            for d in (2 * pair + 1, 2 * pair + 2):
                scale = scale_ref[(d - 1) * BLOCK : d * BLOCK, :]
                spans = spans_of(cols_p, (t,), d)
                moves = spans_of(cols_c, (t,), d)
                inverse = lax.rsqrt(spans[0] * spans[0] + spans[1] * spans[1] + spans[2] * spans[2])
                along = spans[0] * moves[0] + spans[1] * moves[1] + spans[2] * moves[2]
                x = scale * inverse
                u = -(x * inverse * inverse) * along
                xu = xu + fold8(x * u)
                xs.append(x)
                us.append(u)
            at = slice(pair * 2 * BLOCK, (pair + 1) * 2 * BLOCK)
            x, u = jnp.concatenate(xs, 0), jnp.concatenate(us, 0)
            high = x.astype(bf16)
            rest = x - high.astype(f32)
            sq = sq + fold8(x * x)
            pair_lo[at, lanes_x] = rest.astype(bf16)
            pair_hi[at, lanes_x] = (x + pad_one).astype(bf16) if pair == 0 else high
            pair_hi[at, lanes_u], pair_lo[at, lanes_u] = halves(u)
        col_sq.append(jnp.sum(sq, axis=0, keepdims=True))
        col_xu.append(jnp.sum(xu, axis=0, keepdims=True))

    row_sq = []
    for t in range(2):
        for d in range(1, HALF + 1):
            at = slice((d - 1) * BLOCK, d * BLOCK)
            spans = spans_of(rows_w, (t,), d)
            inverse = lax.rsqrt(spans[0] * spans[0] + spans[1] * spans[1] + spans[2] * spans[2])
            x = scale_ref[at, :] * inverse
            row_x[t, at, :] = x
            row_weight[t, at, :] = x * inverse * inverse
        sq = 0.0
        for start in range(0, ROWS, LANES):
            stop = min(start + LANES, ROWS)
            turned = row_x[t, start:stop, :].T
            high = turned.astype(bf16)
            rest = turned - high.astype(f32)
            at = slice(t * LANES, (t + 1) * LANES)
            rowx_hi[at, start:stop] = high
            rowx_lo[at, start:stop] = rest.astype(bf16)
            sq = sq + jnp.sum(turned * turned, axis=1, keepdims=True)
        row_sq.append(sq)

    high, low = rowx_hi[...], rowx_lo[...]
    products = (
        dot_nn(high, pair_hi[...]) + dot_nn(high, pair_lo[...]) + dot_nn(low, pair_hi[...])
    )
    count = 2 * LANES
    gram = products[:, :count] + dot_nn(low, pair_lo[:, :count])
    sq_dist = jnp.concatenate(row_sq, axis=0) + jnp.concatenate(col_sq, axis=1) - 2.0 * gram
    radius = jnp.sqrt(jnp.maximum(sq_dist, 0.0))
    envelope = outer_factor * jnp.exp(-decay_rate * radius)
    direct = envelope * (1.0 + decay_rate * radius)
    bent = (radial_factor * envelope) * (products[:, count:] - jnp.concatenate(col_xu, axis=1))
    high, low = halves(jnp.concatenate([bent, direct], axis=1))
    grads[...] = (
        dot_nt(pair_hi[...], high) + dot_nt(pair_lo[...], high) + dot_nt(pair_hi[...], low)
    )

    for t in range(2):
        lanes = slice(t * LANES, (t + 1) * LANES)
        bend = grads[ATOMS : ATOMS + 1, lanes]
        here = [jnp.zeros((BLOCK, LANES), f32) for _ in range(3)]
        back[...] = jnp.zeros_like(back)
        for d in range(1, HALF + 1):
            at = slice((d - 1) * BLOCK, d * BLOCK)
            pull = row_weight[t, at, :] * (grads[at, lanes] - bend * row_x[t, at, :])
            spans = spans_of(rows_w, (t,), d)
            for k in range(3):
                term = pull * spans[k]
                here[k] = here[k] + term
                back[k, d : d + BLOCK, :] = back[k, d : d + BLOCK, :] + term
        for k in range(3):
            back[k, 0:BLOCK, :] = back[k, 0:BLOCK, :] - here[k]
            back[k, 0:HALF, :] = back[k, 0:HALF, :] + back[k, ATOMS : ATOMS + HALF, :]
            base = t * CART + k * ATOMS
            flat_out[base : base + ATOMS, :] = back[k, 0:ATOMS, :]
    out_ref[...] = flat_out[...].T


def vmem(count):
    return [pl.BlockSpec(memory_space=pltpu.VMEM)] * count


def tile_apply(rows, cols, scale):
    return pl.pallas_call(
        apply_kernel,
        out_shape=jax.ShapeDtypeStruct(rows.shape, f32),
        in_specs=vmem(3),
        out_specs=vmem(1)[0],
        scratch_shapes=[
            pltpu.VMEM((2 * CART, LANES), f32),
            pltpu.VMEM((4 * CART, LANES), f32),
            pltpu.VMEM((2, 3, WRAP, LANES), f32),
            pltpu.VMEM((2, 3, WRAP, LANES), f32),
            pltpu.VMEM((2, 3, WRAP, LANES), f32),
            pltpu.VMEM((ROWS, 4 * LANES), bf16),
            pltpu.VMEM((ROWS, 4 * LANES), bf16),
            pltpu.VMEM((2, ROWS, LANES), f32),
            pltpu.VMEM((2, ROWS, LANES), f32),
            pltpu.VMEM((2 * LANES, ROWS), bf16),
            pltpu.VMEM((2 * LANES, ROWS), bf16),
            pltpu.VMEM((ROWS, 2 * LANES), f32),
            pltpu.VMEM((3, WRAP, LANES), f32),
            pltpu.VMEM((2 * CART, LANES), f32),
        ],
        compiler_params=pltpu.CompilerParams(vmem_limit_bytes=40 * 1024 * 1024),
        cost_estimate=pl.CostEstimate(flops=2_000_000_000, bytes_accessed=2_000_000, transcendentals=1_000_000),
    )(rows, cols, scale)


def scale_table(atom_pairs, pair_scale):
    return pl.pallas_call(
        scale_kernel,
        out_shape=jax.ShapeDtypeStruct((ROWS, LANES), f32),
        in_specs=vmem(2),
        out_specs=vmem(1)[0],
        cost_estimate=pl.CostEstimate(flops=20_000_000, bytes_accessed=700_000, transcendentals=0),
    )(atom_pairs, pair_scale.reshape(1, -1))


def pack(positions, coefficients, row_peers, col_peers):
    half = positions.shape[0] // 2
    return pl.pallas_call(
        pack_kernel,
        out_shape=(
            jax.ShapeDtypeStruct((row_peers, half, 2 * CART), f32),
            jax.ShapeDtypeStruct((col_peers, half, 4 * CART), f32),
        ),
        in_specs=vmem(2),
        out_specs=tuple(vmem(2)),
        cost_estimate=pl.CostEstimate(flops=0, bytes_accessed=400_000, transcendentals=0),
    )(positions, coefficients)


def exchange(value, axis, groups=None):
    return lax.all_to_all(value, axis, split_axis=0, concat_axis=0, tiled=True, axis_index_groups=groups)


def on_device(positions, coefficients, atom_pairs, pair_scale):
    row_count, col_count = lax.axis_size("row"), lax.axis_size("col")
    half = positions.shape[0] // 2
    to_rows, to_cols = pack(positions, coefficients, col_count, row_count // 2)
    scale = scale_table(atom_pairs, pair_scale)
    rows = exchange(to_rows, "col").reshape(-1, 2 * CART)
    same_core = [list(range(core, row_count, 2)) for core in range(2)]
    one_chip = [[n, n + 1] for n in range(0, row_count, 2)]
    cols = exchange(to_cols, "row", same_core).reshape(-1, 4 * CART)
    cols = lax.all_gather(cols, "row", axis=0, tiled=True, axis_index_groups=one_chip)
    partial = tile_apply(rows, cols, scale)
    arrived = exchange(partial.reshape(col_count, half, 2 * CART), "col")
    total = arrived.sum(axis=0)
    return jnp.concatenate([total[:, :CART], total[:, CART:]], axis=0)


def solution(mesh):
    in_specs = (P(("row", "col"), None), P(("row", "col"), None), P(), P())
    out_specs = P(("row", "col"), None)
    return jax.shard_map(
        on_device, mesh=mesh, in_specs=in_specs, out_specs=out_specs, check_vma=False
    )
```

```python
import math

import jax
import jax.numpy as jnp
from jax import lax
from jax.experimental import pallas as pl
from jax.experimental.pallas import tpu as pltpu
from jax.sharding import PartitionSpec as P

ATOMS = 49
HALF = 24
BLOCK = 56
ROWS = HALF * BLOCK
WRAP = 80
CART = 3 * ATOMS
LANES = 128

length_scale = 2.0
decay_rate = math.sqrt(5.0) / length_scale
outer_factor = decay_rate * decay_rate / 3.0
radial_factor = decay_rate * decay_rate
f32 = jnp.float32
bf16 = jnp.bfloat16


def halves(value):
    high = value.astype(bf16)
    return high, (value - high.astype(f32)).astype(bf16)


def dot_nt(a, b):
    return lax.dot_general(a, b, (((1,), (1,)), ((), ())), preferred_element_type=f32)


def dot_nn(a, b):
    return lax.dot_general(a, b, (((1,), (0,)), ((), ())), preferred_element_type=f32)


def spread_scale(pairs_ref, scale_ref, out_ref):
    low, high = pairs_ref[0:1, :], pairs_ref[1:2, :]
    apart = high - low
    near = apart <= HALF
    shift = jnp.where(near, apart, ATOMS - apart) - 1
    start = jnp.where(near, low, high)
    count = low.shape[1]
    atom_ids = lax.broadcasted_iota(jnp.int32, (64, count), 0)
    shift_ids = lax.broadcasted_iota(jnp.int32, (32, count), 0)
    at_atom = jnp.where(atom_ids == start, 1.0, 0.0).astype(bf16)
    scaled = jnp.where(shift_ids == shift, scale_ref[...], 0.0)
    top = scaled.astype(bf16)
    rest = scaled - top.astype(f32)
    middle = rest.astype(bf16)
    bottom = (rest - middle.astype(f32)).astype(bf16)
    table = dot_nt(at_atom, top) + dot_nt(at_atom, middle) + dot_nt(at_atom, bottom)
    for d in range(HALF):
        out_ref[d * BLOCK : (d + 1) * BLOCK, :] = jnp.broadcast_to(
            table[0:BLOCK, d : d + 1], (BLOCK, LANES)
        )


def wrap_rows(flat_ref, start, wrapped_ref, *at):
    for k in range(3):
        base = start + k * ATOMS
        wrapped_ref[(*at, k, slice(0, ATOMS), slice(None))] = flat_ref[base : base + ATOMS, :]
        wrapped_ref[(*at, k, slice(ATOMS, WRAP), slice(None))] = flat_ref[
            base : base + WRAP - ATOMS, :
        ]


def spans_of(wrapped_ref, at, d):
    return [
        wrapped_ref[(*at, k, slice(0, BLOCK), slice(None))]
        - wrapped_ref[(*at, k, slice(d, d + BLOCK), slice(None))]
        for k in range(3)
    ]


def fold8(value):
    total = value[0:8]
    for n in range(1, value.shape[0] // 8):
        total = total + value[8 * n : 8 * n + 8]
    return total


def rows_kernel(
    rows_ref, pairs_ref, pair_scale_ref,
    scale_ref, rows_w, row_x, row_weight, rowx_hi, rowx_lo, row_sq,
    flat_rows,
):
    spread_scale(pairs_ref, pair_scale_ref, scale_ref)
    flat_rows[...] = rows_ref[...].T
    for t in range(2):
        wrap_rows(flat_rows, t * CART, rows_w, t)
    for t in range(2):
        for d in range(1, HALF + 1):
            at = slice((d - 1) * BLOCK, d * BLOCK)
            spans = spans_of(rows_w, (t,), d)
            inverse = lax.rsqrt(spans[0] * spans[0] + spans[1] * spans[1] + spans[2] * spans[2])
            x = scale_ref[at, :] * inverse
            row_x[t, at, :] = x
            row_weight[t, at, :] = x * inverse * inverse
        sq = 0.0
        for start in range(0, ROWS, LANES):
            stop = min(start + LANES, ROWS)
            turned = row_x[t, start:stop, :].T
            high = turned.astype(bf16)
            rest = turned - high.astype(f32)
            at = slice(t * LANES, (t + 1) * LANES)
            rowx_hi[at, start:stop] = high
            rowx_lo[at, start:stop] = rest.astype(bf16)
            sq = sq + jnp.sum(turned * turned, axis=1, keepdims=True)
        row_sq[t * LANES : (t + 1) * LANES, :] = jnp.broadcast_to(sq, (LANES, LANES))


def apply_kernel(
    cols_ref, scale_ref, rows_w, row_x, row_weight, rowx_hi, rowx_lo, row_sq, out_ref,
    flat_cols, cols_p, cols_c, pair_hi, pair_lo, grads, back, flat_out,
):
    flat_cols[...] = cols_ref[...].T
    for t in range(2):
        wrap_rows(flat_cols, t * CART, cols_p, t)
        wrap_rows(flat_cols, (2 + t) * CART, cols_c, t)

    pad_one = (lax.broadcasted_iota(jnp.int32, (2 * BLOCK, LANES), 0) == ATOMS).astype(f32)
    col_sq, col_xu = [], []
    for t in range(2):
        sq, xu = jnp.zeros((8, LANES), f32), jnp.zeros((8, LANES), f32)
        lanes_x = slice(t * LANES, (t + 1) * LANES)
        lanes_u = slice((2 + t) * LANES, (3 + t) * LANES)
        for pair in range(HALF // 2):
            xs, us = [], []
            for d in (2 * pair + 1, 2 * pair + 2):
                scale = scale_ref[(d - 1) * BLOCK : d * BLOCK, :]
                spans = spans_of(cols_p, (t,), d)
                moves = spans_of(cols_c, (t,), d)
                inverse = lax.rsqrt(spans[0] * spans[0] + spans[1] * spans[1] + spans[2] * spans[2])
                along = spans[0] * moves[0] + spans[1] * moves[1] + spans[2] * moves[2]
                x = scale * inverse
                u = -(x * inverse * inverse) * along
                xu = xu + fold8(x * u)
                xs.append(x)
                us.append(u)
            at = slice(pair * 2 * BLOCK, (pair + 1) * 2 * BLOCK)
            x, u = jnp.concatenate(xs, 0), jnp.concatenate(us, 0)
            high = x.astype(bf16)
            rest = x - high.astype(f32)
            sq = sq + fold8(x * x)
            pair_lo[at, lanes_x] = rest.astype(bf16)
            pair_hi[at, lanes_x] = (x + pad_one).astype(bf16) if pair == 0 else high
            pair_hi[at, lanes_u], pair_lo[at, lanes_u] = halves(u)
        col_sq.append(jnp.sum(sq, axis=0, keepdims=True))
        col_xu.append(jnp.sum(xu, axis=0, keepdims=True))

    high, low = rowx_hi[...], rowx_lo[...]
    products = (
        dot_nn(high, pair_hi[...]) + dot_nn(high, pair_lo[...]) + dot_nn(low, pair_hi[...])
    )
    count = 2 * LANES
    gram = products[:, :count] + dot_nn(low, pair_lo[:, :count])
    sq_dist = row_sq[:, 0:1] + jnp.concatenate(col_sq, axis=1) - 2.0 * gram
    radius = jnp.sqrt(jnp.maximum(sq_dist, 0.0))
    envelope = outer_factor * jnp.exp(-decay_rate * radius)
    direct = envelope * (1.0 + decay_rate * radius)
    bent = (radial_factor * envelope) * (products[:, count:] - jnp.concatenate(col_xu, axis=1))
    high, low = halves(jnp.concatenate([bent, direct], axis=1))
    grads[...] = (
        dot_nt(pair_hi[...], high) + dot_nt(pair_lo[...], high) + dot_nt(pair_hi[...], low)
    )

    for t in range(2):
        lanes = slice(t * LANES, (t + 1) * LANES)
        bend = grads[ATOMS : ATOMS + 1, lanes]
        here = [jnp.zeros((BLOCK, LANES), f32) for _ in range(3)]
        back[...] = jnp.zeros_like(back)
        for d in range(1, HALF + 1):
            at = slice((d - 1) * BLOCK, d * BLOCK)
            pull = row_weight[t, at, :] * (grads[at, lanes] - bend * row_x[t, at, :])
            spans = spans_of(rows_w, (t,), d)
            for k in range(3):
                term = pull * spans[k]
                here[k] = here[k] + term
                back[k, d : d + BLOCK, :] = back[k, d : d + BLOCK, :] + term
        for k in range(3):
            back[k, 0:BLOCK, :] = back[k, 0:BLOCK, :] - here[k]
            back[k, 0:HALF, :] = back[k, 0:HALF, :] + back[k, ATOMS : ATOMS + HALF, :]
            base = t * CART + k * ATOMS
            flat_out[base : base + ATOMS, :] = back[k, 0:ATOMS, :]
    out_ref[...] = flat_out[...].T


def vmem(count):
    return [pl.BlockSpec(memory_space=pltpu.VMEM)] * count


def shape(*dims, kind=f32):
    return jax.ShapeDtypeStruct(dims, kind)


params = pltpu.CompilerParams(vmem_limit_bytes=20 * 1024 * 1024)


def row_terms(rows, atom_pairs, pair_scale):
    return pl.pallas_call(
        rows_kernel,
        out_shape=(
            shape(ROWS, LANES),
            shape(2, 3, WRAP, LANES),
            shape(2, ROWS, LANES),
            shape(2, ROWS, LANES),
            shape(2 * LANES, ROWS, kind=bf16),
            shape(2 * LANES, ROWS, kind=bf16),
            shape(2 * LANES, LANES),
        ),
        in_specs=vmem(3),
        out_specs=tuple(vmem(7)),
        scratch_shapes=[pltpu.VMEM((2 * CART, LANES), f32)],
        compiler_params=params,
        cost_estimate=pl.CostEstimate(
            flops=40_000_000, bytes_accessed=6_000_000, transcendentals=300_000
        ),
    )(rows, atom_pairs, pair_scale.reshape(1, -1))


def tile_apply(cols, terms):
    return pl.pallas_call(
        apply_kernel,
        out_shape=shape(LANES, 2 * CART),
        in_specs=vmem(1 + len(terms)),
        out_specs=vmem(1)[0],
        scratch_shapes=[
            pltpu.VMEM((4 * CART, LANES), f32),
            pltpu.VMEM((2, 3, WRAP, LANES), f32),
            pltpu.VMEM((2, 3, WRAP, LANES), f32),
            pltpu.VMEM((ROWS, 4 * LANES), bf16),
            pltpu.VMEM((ROWS, 4 * LANES), bf16),
            pltpu.VMEM((ROWS, 2 * LANES), f32),
            pltpu.VMEM((3, WRAP, LANES), f32),
            pltpu.VMEM((2 * CART, LANES), f32),
        ],
        compiler_params=params,
        cost_estimate=pl.CostEstimate(
            flops=2_000_000_000, bytes_accessed=6_000_000, transcendentals=500_000
        ),
    )(cols, *terms)


def side_by_side(value):
    half = value.shape[0] // 2
    return jnp.concatenate([value[:half], value[half:]], axis=1)


def exchange(value, axis):
    return lax.all_to_all(value, axis, split_axis=0, concat_axis=0, tiled=True)


def from_everyone(value, axis):
    copies = jnp.broadcast_to(value, (lax.axis_size(axis), *value.shape))
    return exchange(copies, axis).reshape(-1, value.shape[1])


def on_device(positions, coefficients, atom_pairs, pair_scale):
    packed = jnp.concatenate([side_by_side(positions), side_by_side(coefficients)], axis=1)
    rows = from_everyone(packed[:, : 2 * CART], "row")
    rows, packed = lax.optimization_barrier((rows, packed))
    cols = from_everyone(packed, "col")
    partial = tile_apply(cols, row_terms(rows, atom_pairs, pair_scale))
    arrived = exchange(partial.reshape(lax.axis_size("row"), -1, 2 * CART), "row")
    total = arrived.sum(axis=0)
    return jnp.concatenate([total[:, :CART], total[:, CART:]], axis=0)


def solution(mesh):
    in_specs = (P(("row", "col"), None), P(("row", "col"), None), P(), P())
    out_specs = P(("row", "col"), None)
    return jax.shard_map(
        on_device, mesh=mesh, in_specs=in_specs, out_specs=out_specs, check_vma=False
    )
```

```python
import math

import jax
import jax.numpy as jnp
from jax import lax
from jax.experimental import pallas as pl
from jax.experimental.pallas import tpu as pltpu
from jax.sharding import PartitionSpec as P

ATOMS = 49
HALF = 24
BLOCK = 56
ROWS = HALF * BLOCK
WRAP = 80
CART = 3 * ATOMS
LANES = 128

length_scale = 2.0
decay_rate = math.sqrt(5.0) / length_scale
outer_factor = decay_rate * decay_rate / 3.0
radial_factor = decay_rate * decay_rate
f32 = jnp.float32
bf16 = jnp.bfloat16


def halves(value):
    high = value.astype(bf16)
    return high, (value - high.astype(f32)).astype(bf16)


def dot_nt(a, b):
    return lax.dot_general(a, b, (((1,), (1,)), ((), ())), preferred_element_type=f32)


def dot_nn(a, b):
    return lax.dot_general(a, b, (((1,), (0,)), ((), ())), preferred_element_type=f32)


def spread_scale(pairs_ref, scale_ref, out_ref):
    low, high = pairs_ref[0:1, :], pairs_ref[1:2, :]
    apart = high - low
    near = apart <= HALF
    shift = jnp.where(near, apart, ATOMS - apart) - 1
    start = jnp.where(near, low, high)
    count = low.shape[1]
    atom_ids = lax.broadcasted_iota(jnp.int32, (64, count), 0)
    shift_ids = lax.broadcasted_iota(jnp.int32, (32, count), 0)
    at_atom = jnp.where(atom_ids == start, 1.0, 0.0).astype(bf16)
    scaled = jnp.where(shift_ids == shift, scale_ref[...], 0.0)
    top = scaled.astype(bf16)
    rest = scaled - top.astype(f32)
    middle = rest.astype(bf16)
    bottom = (rest - middle.astype(f32)).astype(bf16)
    table = dot_nt(at_atom, top) + dot_nt(at_atom, middle) + dot_nt(at_atom, bottom)
    for d in range(HALF):
        out_ref[d * BLOCK : (d + 1) * BLOCK, :] = jnp.broadcast_to(
            table[0:BLOCK, d : d + 1], (BLOCK, LANES)
        )


def wrap_rows(flat_ref, start, wrapped_ref, *at):
    for k in range(3):
        base = start + k * ATOMS
        wrapped_ref[(*at, k, slice(0, ATOMS), slice(None))] = flat_ref[base : base + ATOMS, :]
        wrapped_ref[(*at, k, slice(ATOMS, WRAP), slice(None))] = flat_ref[
            base : base + WRAP - ATOMS, :
        ]


def spans_of(wrapped_ref, at, d):
    return [
        wrapped_ref[(*at, k, slice(0, BLOCK), slice(None))]
        - wrapped_ref[(*at, k, slice(d, d + BLOCK), slice(None))]
        for k in range(3)
    ]


def fold8(value):
    total = value[0:8]
    for n in range(1, value.shape[0] // 8):
        total = total + value[8 * n : 8 * n + 8]
    return total


def apply_kernel(
    rows_ref, cols_ref, pairs_ref, pair_scale_ref, out_ref,
    scale_ref, flat_rows, flat_cols, rows_w, cols_p, cols_c, pair_hi, pair_lo, row_x, row_weight,
    rowx_hi, rowx_lo, grads, back, flat_out,
):
    spread_scale(pairs_ref, pair_scale_ref, scale_ref)
    flat_cols[...] = cols_ref[...].T
    flat_rows[...] = rows_ref[...].T
    for t in range(2):
        wrap_rows(flat_cols, t * CART, cols_p, t)
        wrap_rows(flat_cols, (2 + t) * CART, cols_c, t)
        wrap_rows(flat_rows, t * CART, rows_w, t)

    pad_one = (lax.broadcasted_iota(jnp.int32, (2 * BLOCK, LANES), 0) == ATOMS).astype(f32)
    col_sq, col_xu = [], []
    for t in range(2):
        sq, xu = jnp.zeros((8, LANES), f32), jnp.zeros((8, LANES), f32)
        lanes_x = slice(t * LANES, (t + 1) * LANES)
        lanes_u = slice((2 + t) * LANES, (3 + t) * LANES)
        for pair in range(HALF // 2):
            xs, us = [], []
            for d in (2 * pair + 1, 2 * pair + 2):
                scale = scale_ref[(d - 1) * BLOCK : d * BLOCK, :]
                spans = spans_of(cols_p, (t,), d)
                moves = spans_of(cols_c, (t,), d)
                inverse = lax.rsqrt(spans[0] * spans[0] + spans[1] * spans[1] + spans[2] * spans[2])
                along = spans[0] * moves[0] + spans[1] * moves[1] + spans[2] * moves[2]
                x = scale * inverse
                u = -(x * inverse * inverse) * along
                xu = xu + fold8(x * u)
                xs.append(x)
                us.append(u)
            at = slice(pair * 2 * BLOCK, (pair + 1) * 2 * BLOCK)
            x, u = jnp.concatenate(xs, 0), jnp.concatenate(us, 0)
            high = x.astype(bf16)
            rest = x - high.astype(f32)
            sq = sq + fold8(x * x)
            pair_lo[at, lanes_x] = rest.astype(bf16)
            pair_hi[at, lanes_x] = (x + pad_one).astype(bf16) if pair == 0 else high
            pair_hi[at, lanes_u], pair_lo[at, lanes_u] = halves(u)
        col_sq.append(jnp.sum(sq, axis=0, keepdims=True))
        col_xu.append(jnp.sum(xu, axis=0, keepdims=True))

    row_sq = []
    for t in range(2):
        for d in range(1, HALF + 1):
            at = slice((d - 1) * BLOCK, d * BLOCK)
            spans = spans_of(rows_w, (t,), d)
            inverse = lax.rsqrt(spans[0] * spans[0] + spans[1] * spans[1] + spans[2] * spans[2])
            x = scale_ref[at, :] * inverse
            row_x[t, at, :] = x
            row_weight[t, at, :] = x * inverse * inverse
        sq = 0.0
        for start in range(0, ROWS, LANES):
            stop = min(start + LANES, ROWS)
            turned = row_x[t, start:stop, :].T
            high = turned.astype(bf16)
            rest = turned - high.astype(f32)
            at = slice(t * LANES, (t + 1) * LANES)
            rowx_hi[at, start:stop] = high
            rowx_lo[at, start:stop] = rest.astype(bf16)
            sq = sq + jnp.sum(turned * turned, axis=1, keepdims=True)
        row_sq.append(sq)

    high, low = rowx_hi[...], rowx_lo[...]
    products = (
        dot_nn(high, pair_hi[...]) + dot_nn(high, pair_lo[...]) + dot_nn(low, pair_hi[...])
    )
    count = 2 * LANES
    gram = products[:, :count] + dot_nn(low, pair_lo[:, :count])
    sq_dist = jnp.concatenate(row_sq, axis=0) + jnp.concatenate(col_sq, axis=1) - 2.0 * gram
    radius = jnp.sqrt(jnp.maximum(sq_dist, 0.0))
    envelope = outer_factor * jnp.exp(-decay_rate * radius)
    direct = envelope * (1.0 + decay_rate * radius)
    bent = (radial_factor * envelope) * (products[:, count:] - jnp.concatenate(col_xu, axis=1))
    high, low = halves(jnp.concatenate([bent, direct], axis=1))
    grads[...] = (
        dot_nt(pair_hi[...], high) + dot_nt(pair_lo[...], high) + dot_nt(pair_hi[...], low)
    )

    for t in range(2):
        lanes = slice(t * LANES, (t + 1) * LANES)
        bend = grads[ATOMS : ATOMS + 1, lanes]
        here = [jnp.zeros((BLOCK, LANES), f32) for _ in range(3)]
        back[...] = jnp.zeros_like(back)
        for d in range(1, HALF + 1):
            at = slice((d - 1) * BLOCK, d * BLOCK)
            pull = row_weight[t, at, :] * (grads[at, lanes] - bend * row_x[t, at, :])
            spans = spans_of(rows_w, (t,), d)
            for k in range(3):
                term = pull * spans[k]
                here[k] = here[k] + term
                back[k, d : d + BLOCK, :] = back[k, d : d + BLOCK, :] + term
        for k in range(3):
            back[k, 0:BLOCK, :] = back[k, 0:BLOCK, :] - here[k]
            back[k, 0:HALF, :] = back[k, 0:HALF, :] + back[k, ATOMS : ATOMS + HALF, :]
            base = t * CART + k * ATOMS
            flat_out[base : base + ATOMS, :] = back[k, 0:ATOMS, :]
    out_ref[...] = flat_out[...].T


def vmem(count):
    return [pl.BlockSpec(memory_space=pltpu.VMEM)] * count


def tile_apply(rows, cols, atom_pairs, pair_scale):
    return pl.pallas_call(
        apply_kernel,
        out_shape=jax.ShapeDtypeStruct(rows.shape, f32),
        in_specs=vmem(4),
        out_specs=vmem(1)[0],
        scratch_shapes=[
            pltpu.VMEM((ROWS, LANES), f32),
            pltpu.VMEM((2 * CART, LANES), f32),
            pltpu.VMEM((4 * CART, LANES), f32),
            pltpu.VMEM((2, 3, WRAP, LANES), f32),
            pltpu.VMEM((2, 3, WRAP, LANES), f32),
            pltpu.VMEM((2, 3, WRAP, LANES), f32),
            pltpu.VMEM((ROWS, 4 * LANES), bf16),
            pltpu.VMEM((ROWS, 4 * LANES), bf16),
            pltpu.VMEM((2, ROWS, LANES), f32),
            pltpu.VMEM((2, ROWS, LANES), f32),
            pltpu.VMEM((2 * LANES, ROWS), bf16),
            pltpu.VMEM((2 * LANES, ROWS), bf16),
            pltpu.VMEM((ROWS, 2 * LANES), f32),
            pltpu.VMEM((3, WRAP, LANES), f32),
            pltpu.VMEM((2 * CART, LANES), f32),
        ],
        compiler_params=pltpu.CompilerParams(vmem_limit_bytes=32 * 1024 * 1024),
        cost_estimate=pl.CostEstimate(
            flops=2_000_000_000, bytes_accessed=2_000_000, transcendentals=1_000_000
        ),
    )(rows, cols, atom_pairs, pair_scale.reshape(1, -1))


def side_by_side(value):
    half = value.shape[0] // 2
    return jnp.concatenate([value[:half], value[half:]], axis=1)


def exchange(value, axis):
    return lax.all_to_all(value, axis, split_axis=0, concat_axis=0, tiled=True)


def from_everyone(value, axis):
    copies = jnp.broadcast_to(value, (lax.axis_size(axis), *value.shape))
    return exchange(copies, axis).reshape(-1, value.shape[1])


def on_device(positions, coefficients, atom_pairs, pair_scale):
    packed = jnp.concatenate([side_by_side(positions), side_by_side(coefficients)], axis=1)
    chained = (packed[:, : 2 * CART], packed, atom_pairs, pair_scale)
    rows, *rest = lax.optimization_barrier(chained)
    rows, cols, *rest = lax.optimization_barrier((from_everyone(rows, "row"), *rest))
    chained = lax.optimization_barrier((rows, from_everyone(cols, "col"), *rest))
    partial = tile_apply(*chained)
    arrived = exchange(partial.reshape(lax.axis_size("row"), -1, 2 * CART), "row")
    total = arrived.sum(axis=0)
    return jnp.concatenate([total[:, :CART], total[:, CART:]], axis=0)


def solution(mesh):
    in_specs = (P(("row", "col"), None), P(("row", "col"), None), P(), P())
    out_specs = P(("row", "col"), None)
    return jax.shard_map(
        on_device, mesh=mesh, in_specs=in_specs, out_specs=out_specs, check_vma=False
    )
```

```python
import math

import jax
import jax.numpy as jnp
from jax import lax
from jax.experimental import pallas as pl
from jax.experimental.pallas import tpu as pltpu
from jax.sharding import PartitionSpec as P

ATOMS = 49
HALF = 24
BLOCK = 48
LAST = HALF * BLOCK
PAIRS = LAST + HALF
ROWS = PAIRS + 8
KDIM = ROWS
WRAP = 72
CART = 3 * ATOMS
LANES = 128

length_scale = 2.0
decay_rate = math.sqrt(5.0) / length_scale
outer_factor = decay_rate * decay_rate / 3.0
radial_factor = decay_rate * decay_rate
f32 = jnp.float32
bf16 = jnp.bfloat16


def halves(value):
    high = value.astype(bf16)
    return high, (value - high.astype(f32)).astype(bf16)


def dot_nt(a, b):
    return lax.dot_general(a, b, (((1,), (1,)), ((), ())), preferred_element_type=f32)


def dot_nn(a, b):
    return lax.dot_general(a, b, (((1,), (0,)), ((), ())), preferred_element_type=f32)


def spread_scale(pairs_ref, scale_ref, out_ref):
    low, high = pairs_ref[0:1, :], pairs_ref[1:2, :]
    apart = high - low
    near = apart <= HALF
    shift = jnp.where(near, apart, ATOMS - apart) - 1
    start = jnp.where(near, low, high)
    count = low.shape[1]
    atom_ids = lax.broadcasted_iota(jnp.int32, (64, count), 0)
    shift_ids = lax.broadcasted_iota(jnp.int32, (32, count), 0)
    at_atom = jnp.where(atom_ids == start, 1.0, 0.0).astype(bf16)
    scaled = jnp.where(shift_ids == shift, scale_ref[...], 0.0)
    top = scaled.astype(bf16)
    rest = scaled - top.astype(f32)
    middle = rest.astype(bf16)
    bottom = (rest - middle.astype(f32)).astype(bf16)
    table = dot_nt(at_atom, top) + dot_nt(at_atom, middle) + dot_nt(at_atom, bottom)
    for d in range(HALF):
        out_ref[d * BLOCK : (d + 1) * BLOCK, :] = jnp.broadcast_to(
            table[0:BLOCK, d : d + 1], (BLOCK, LANES)
        )
    last = jnp.where(start == ATOMS - 1, scaled, 0.0)
    last = jnp.sum(last[0:HALF], axis=1, keepdims=True)
    out_ref[LAST:PAIRS, :] = jnp.broadcast_to(last, (HALF, LANES))


def wrap_rows(flat_ref, start, wrapped_ref, *at):
    for k in range(3):
        base = start + k * ATOMS
        wrapped_ref[(*at, k, slice(0, ATOMS), slice(None))] = flat_ref[base : base + ATOMS, :]
        wrapped_ref[(*at, k, slice(ATOMS, WRAP), slice(None))] = flat_ref[
            base : base + WRAP - ATOMS, :
        ]


def spans_of(wrapped_ref, at, d):
    if d == 0:
        here, there = slice(ATOMS - 1, ATOMS), slice(0, HALF)
    else:
        here, there = slice(0, BLOCK), slice(d, d + BLOCK)
    return [
        wrapped_ref[(*at, k, here, slice(None))] - wrapped_ref[(*at, k, there, slice(None))]
        for k in range(3)
    ]


def rows_of(d):
    return slice((d - 1) * BLOCK, d * BLOCK) if d else slice(LAST, PAIRS)


CHUNKS = ((0, ROWS),)
PARTS = ((768, ROWS), (0, 384), (384, 768))
separations = (*range(1, HALF + 1), 0)


def fold8(value):
    total = value[0:8]
    for n in range(1, value.shape[0] // 8):
        total = total + value[8 * n : 8 * n + 8]
    return total


def rows_kernel(
    rows_ref, pairs_ref, pair_scale_ref,
    scale_ref, rows_w, rowx_hi, rowx_lo, row_sq,
    flat_rows, row_x,
):
    spread_scale(pairs_ref, pair_scale_ref, scale_ref)
    flat_rows[...] = rows_ref[...].T
    for t in range(2):
        wrap_rows(flat_rows, t * CART, rows_w, t)
    nothing = jnp.zeros((8, LANES), f32)
    for t in range(2):
        for d in separations:
            at = rows_of(d)
            spans = spans_of(rows_w, (t,), d)
            inverse = lax.rsqrt(spans[0] * spans[0] + spans[1] * spans[1] + spans[2] * spans[2])
            x = scale_ref[at, :] * inverse
            row_x[t, at, :] = x
        row_x[t, PAIRS:ROWS, :] = nothing
        sq = 0.0
        for start in range(0, ROWS, LANES):
            stop = min(start + LANES, ROWS)
            turned = row_x[t, start:stop, :].T
            high = turned.astype(bf16)
            rest = turned - high.astype(f32)
            at = slice(t * LANES, (t + 1) * LANES)
            rowx_hi[at, start:stop] = high
            rowx_lo[at, start:stop] = rest.astype(bf16)
            sq = sq + jnp.sum(turned * turned, axis=1, keepdims=True)
        row_sq[t * LANES : (t + 1) * LANES, :] = jnp.broadcast_to(sq, (LANES, LANES))


def apply_kernel(
    cols_ref, scale_ref, rows_w, rowx_hi, rowx_lo, row_sq, out_ref,
    flat_cols, cols_p, cols_c, pair_hi, pair_lo, grads, back, flat_out,
):
    flat_cols[...] = cols_ref[...].T
    for t in range(2):
        wrap_rows(flat_cols, t * CART, cols_p, t)
        wrap_rows(flat_cols, (2 + t) * CART, cols_c, t)

    extra = jnp.where(lax.broadcasted_iota(jnp.int32, (8, LANES), 0) == 0, 1.0, 0.0)
    nothing = jnp.zeros((8, LANES), f32)
    col_sq, col_xu = [], []
    for t in range(2):
        sq, xu = nothing, nothing
        lanes_x = slice(t * LANES, (t + 1) * LANES)
        lanes_u = slice((2 + t) * LANES, (3 + t) * LANES)
        for d in separations:
            spans = spans_of(cols_p, (t,), d)
            moves = spans_of(cols_c, (t,), d)
            inverse = lax.rsqrt(spans[0] * spans[0] + spans[1] * spans[1] + spans[2] * spans[2])
            along = spans[0] * moves[0] + spans[1] * moves[1] + spans[2] * moves[2]
            x = scale_ref[rows_of(d), :] * inverse
            u = -(x * inverse * inverse) * along
            sq = sq + fold8(x * x)
            xu = xu + fold8(x * u)
            at = rows_of(d)
            if d == 0:
                x, u = jnp.concatenate([x, extra], 0), jnp.concatenate([u, nothing], 0)
                at = slice(LAST, ROWS)
            pair_hi[at, lanes_x], pair_lo[at, lanes_x] = halves(x)
            pair_hi[at, lanes_u], pair_lo[at, lanes_u] = halves(u)
        col_sq.append(jnp.sum(sq, axis=0, keepdims=True))
        col_xu.append(jnp.sum(xu, axis=0, keepdims=True))

    count = 2 * LANES
    products, low_low = 0.0, 0.0
    for start, stop in CHUNKS:
        at = slice(start, stop)
        high, low = rowx_hi[:, at], rowx_lo[:, at]
        products = (
            products
            + dot_nn(high, pair_hi[at, :])
            + dot_nn(high, pair_lo[at, :])
            + dot_nn(low, pair_hi[at, :])
        )
        low_low = low_low + dot_nn(low, pair_lo[at, :count])
    gram = products[:, :count] + low_low
    sq_dist = row_sq[:, 0:1] + jnp.concatenate(col_sq, axis=1) - 2.0 * gram
    radius = jnp.sqrt(jnp.maximum(sq_dist, 0.0))
    envelope = outer_factor * jnp.exp(-decay_rate * radius)
    direct = envelope * (1.0 + decay_rate * radius)
    bent = (radial_factor * envelope) * (products[:, count:] - jnp.concatenate(col_xu, axis=1))
    high, low = halves(jnp.concatenate([bent, direct], axis=1))
    for start, stop in PARTS:
        part_hi, part_lo = pair_hi[start:stop, :], pair_lo[start:stop, :]
        grads[start:stop, :] = (
            dot_nt(part_hi, high) + dot_nt(part_lo, high) + dot_nt(part_hi, low)
        )

    for t in range(2):
        lanes = slice(t * LANES, (t + 1) * LANES)
        bend = grads[PAIRS : PAIRS + 1, lanes]

        def terms_of(d):
            at = rows_of(d)
            spans = spans_of(rows_w, (t,), d)
            inverse = lax.rsqrt(spans[0] * spans[0] + spans[1] * spans[1] + spans[2] * spans[2])
            x = scale_ref[at, :] * inverse
            pull = (x * inverse * inverse) * (grads[at, lanes] - bend * x)
            return [pull * span for span in spans]

        back[t] = jnp.zeros(back.shape[1:], f32)
        for k, term in enumerate(terms_of(0)):
            back[t, k, 0:HALF, :] = term
            back[t, k, ATOMS - 1 : ATOMS, :] = -jnp.sum(term, axis=0, keepdims=True)
        here = [jnp.zeros((BLOCK, LANES), f32) for _ in range(3)]
        for shift in range(1, 9):
            there = [None] * 3
            for step in range(3):
                for k, term in enumerate(terms_of(shift + 8 * step)):
                    here[k] = here[k] + term
                    if step == 0:
                        there[k] = [term[8 * n : 8 * n + 8] for n in range(BLOCK // 8)]
                    else:
                        for n in range(BLOCK // 8):
                            piece = term[8 * n : 8 * n + 8]
                            if step + n < len(there[k]):
                                there[k][step + n] = there[k][step + n] + piece
                            else:
                                there[k].append(piece)
            for k in range(3):
                total = jnp.concatenate(there[k], axis=0)
                at = slice(shift, shift + total.shape[0])
                back[t, k, at, :] = back[t, k, at, :] + total
        for k in range(3):
            back[t, k, 0:BLOCK, :] = back[t, k, 0:BLOCK, :] - here[k]
            back[t, k, 0 : WRAP - ATOMS, :] = back[t, k, 0 : WRAP - ATOMS, :] + back[t, k, ATOMS:WRAP, :]
            base = t * CART + k * ATOMS
            flat_out[base : base + ATOMS, :] = back[t, k, 0:ATOMS, :]
    out_ref[...] = flat_out[...].T


def vmem(count):
    return [pl.BlockSpec(memory_space=pltpu.VMEM)] * count


def shape(*dims, kind=f32):
    return jax.ShapeDtypeStruct(dims, kind)


params = pltpu.CompilerParams(vmem_limit_bytes=12 * 1024 * 1024)


def row_terms(rows, atom_pairs, pair_scale):
    return pl.pallas_call(
        rows_kernel,
        out_shape=(
            shape(ROWS, LANES),
            shape(2, 3, WRAP, LANES),
            shape(2 * LANES, KDIM, kind=bf16),
            shape(2 * LANES, KDIM, kind=bf16),
            shape(2 * LANES, LANES),
        ),
        in_specs=vmem(3),
        out_specs=tuple(vmem(5)),
        scratch_shapes=[pltpu.VMEM((2 * CART, LANES), f32), pltpu.VMEM((2, ROWS, LANES), f32)],
        compiler_params=params,
        cost_estimate=pl.CostEstimate(
            flops=40_000_000, bytes_accessed=6_000_000, transcendentals=300_000
        ),
    )(rows, atom_pairs, pair_scale.reshape(1, -1))


def cols_apply(cols, terms):
    return pl.pallas_call(
        apply_kernel,
        out_shape=shape(LANES, 2 * CART),
        in_specs=vmem(1 + len(terms)),
        out_specs=vmem(1)[0],
        scratch_shapes=[
            pltpu.VMEM((4 * CART, LANES), f32),
            pltpu.VMEM((2, 3, WRAP, LANES), f32),
            pltpu.VMEM((2, 3, WRAP, LANES), f32),
            pltpu.VMEM((KDIM, 4 * LANES), bf16),
            pltpu.VMEM((KDIM, 4 * LANES), bf16),
            pltpu.VMEM((ROWS, 2 * LANES), f32),
            pltpu.VMEM((2, 3, WRAP, LANES), f32),
            pltpu.VMEM((2 * CART, LANES), f32),
        ],
        compiler_params=params,
        cost_estimate=pl.CostEstimate(
            flops=2_000_000_000, bytes_accessed=6_000_000, transcendentals=500_000
        ),
    )(cols, *terms)


def tile_apply(rows, cols, atom_pairs, pair_scale):
    return cols_apply(cols, row_terms(rows, atom_pairs, pair_scale))


def side_by_side(value):
    half = value.shape[0] // 2
    return jnp.concatenate([value[:half], value[half:]], axis=1)


def exchange(value, axis):
    return lax.all_to_all(value, axis, split_axis=0, concat_axis=0, tiled=True)


def from_everyone(value, axis):
    copies = jnp.broadcast_to(value, (lax.axis_size(axis), *value.shape))
    return exchange(copies, axis).reshape(-1, value.shape[1])


def on_device(positions, coefficients, atom_pairs, pair_scale):
    packed = jnp.concatenate([side_by_side(positions), side_by_side(coefficients)], axis=1)
    rows, *rest = lax.optimization_barrier((packed[:, : 2 * CART], packed, atom_pairs, pair_scale))
    chained = lax.optimization_barrier((from_everyone(rows, "row"), *rest))
    rows, packed, atom_pairs, pair_scale = chained
    cols = from_everyone(packed, "col")
    partial = tile_apply(rows, cols, atom_pairs, pair_scale)
    arrived = exchange(partial.reshape(lax.axis_size("row"), -1, 2 * CART), "row")
    total = arrived.sum(axis=0)
    return jnp.concatenate([total[:, :CART], total[:, CART:]], axis=0)


def solution(mesh):
    in_specs = (P(("row", "col"), None), P(("row", "col"), None), P(), P())
    out_specs = P(("row", "col"), None)
    return jax.shard_map(
        on_device, mesh=mesh, in_specs=in_specs, out_specs=out_specs, check_vma=False
    )
```

```python
import functools
import math

import jax
import jax.numpy as jnp
from jax import lax
from jax.experimental import pallas as pl
from jax.experimental.pallas import tpu as pltpu
from jax.sharding import PartitionSpec as P

ATOMS = 49
HALF = 24
BLOCK = 48
LAST = HALF * BLOCK
PAIRS = LAST + HALF
ROWS = PAIRS + 8
KDIM = ROWS
HALF_ROWS = 8
WRAP = 72
CART = 3 * ATOMS
LANES = 128

length_scale = 2.0
decay_rate = math.sqrt(5.0) / length_scale
outer_factor = decay_rate * decay_rate / 3.0
radial_factor = decay_rate * decay_rate
f32 = jnp.float32
bf16 = jnp.bfloat16


def halves(value):
    high = value.astype(bf16)
    return high, (value - high.astype(f32)).astype(bf16)


def dot_nt(a, b):
    return lax.dot_general(a, b, (((1,), (1,)), ((), ())), preferred_element_type=f32)


def dot_nn(a, b):
    return lax.dot_general(a, b, (((1,), (0,)), ((), ())), preferred_element_type=f32)


def spread_scale(pairs_ref, scale_ref, out_ref):
    low, high = pairs_ref[0:1, :], pairs_ref[1:2, :]
    apart = high - low
    near = apart <= HALF
    shift = jnp.where(near, apart, ATOMS - apart) - 1
    start = jnp.where(near, low, high)
    count = low.shape[1]
    atom_ids = lax.broadcasted_iota(jnp.int32, (64, count), 0)
    shift_ids = lax.broadcasted_iota(jnp.int32, (32, count), 0)
    at_atom = jnp.where(atom_ids == start, 1.0, 0.0).astype(bf16)
    scaled = jnp.where(shift_ids == shift, scale_ref[...], 0.0)
    top = scaled.astype(bf16)
    rest = scaled - top.astype(f32)
    middle = rest.astype(bf16)
    bottom = (rest - middle.astype(f32)).astype(bf16)
    table = dot_nt(at_atom, top) + dot_nt(at_atom, middle) + dot_nt(at_atom, bottom)
    for d in range(HALF):
        out_ref[rows_of(d + 1), :] = jnp.broadcast_to(
            table[0:BLOCK, d : d + 1], (BLOCK, LANES)
        )
    last = jnp.where(start == ATOMS - 1, scaled, 0.0)
    last = jnp.sum(last[0:HALF], axis=1, keepdims=True)
    out_ref[LAST:PAIRS, :] = jnp.broadcast_to(last, (HALF, LANES))


def wrap_rows(flat_ref, start, wrapped_ref, *at):
    for k in range(3):
        base = start + k * ATOMS
        wrapped_ref[(*at, k, slice(0, ATOMS), slice(None))] = flat_ref[base : base + ATOMS, :]
        wrapped_ref[(*at, k, slice(ATOMS, WRAP), slice(None))] = flat_ref[
            base : base + WRAP - ATOMS, :
        ]


def spans_of(wrapped_ref, at, d):
    if d == 0:
        here, there = slice(ATOMS - 1, ATOMS), slice(0, HALF)
    else:
        here, there = slice(0, BLOCK), slice(d, d + BLOCK)
    return [
        wrapped_ref[(*at, k, here, slice(None))] - wrapped_ref[(*at, k, there, slice(None))]
        for k in range(3)
    ]


def rows_of(d):
    if d == 0:
        return slice(LAST, PAIRS)
    place = 3 * ((d - 1) % 8) + (d - 1) // 8
    return slice(place * BLOCK, (place + 1) * BLOCK)


GROUP = 3 * BLOCK
PARTS = ((7, 9), (1, 3), (3, 5), (5, 7))
separations = (*range(1, HALF + 1), 0)


def fold8(value):
    total = value[0:8]
    for n in range(1, value.shape[0] // 8):
        total = total + value[8 * n : 8 * n + 8]
    return total


def rows_kernel(
    rows_ref, pairs_ref, pair_scale_ref,
    scale_ref, rows_w, rowx_hi, rowx_lo, row_sq,
    flat_rows, row_x,
):
    spread_scale(pairs_ref, pair_scale_ref, scale_ref)
    flat_rows[...] = rows_ref[...].T
    for t in range(2):
        wrap_rows(flat_rows, t * CART, rows_w, t)
    nothing = jnp.zeros((8, LANES), f32)
    for t in range(2):
        for d in separations:
            at = rows_of(d)
            spans = spans_of(rows_w, (t,), d)
            inverse = lax.rsqrt(spans[0] * spans[0] + spans[1] * spans[1] + spans[2] * spans[2])
            x = scale_ref[at, :] * inverse
            row_x[t, at, :] = x
        row_x[t, PAIRS:ROWS, :] = nothing
        sq = 0.0
        for start in range(0, ROWS, LANES):
            stop = min(start + LANES, ROWS)
            turned = row_x[t, start:stop, :].T
            high = turned.astype(bf16)
            rest = turned - high.astype(f32)
            at = slice(t * LANES, (t + 1) * LANES)
            rowx_hi[at, start:stop] = high
            rowx_lo[at, start:stop] = rest.astype(bf16)
            sq = sq + jnp.sum(turned * turned, axis=1, keepdims=True)
        row_sq[t * LANES : (t + 1) * LANES, :] = jnp.broadcast_to(sq, (LANES, LANES))


def apply_kernel(
    place, cols_ref, scale_ref, rows_w, rowx_hi, rowx_lo, row_sq, out_ref,
    flat_cols, cols_p, cols_c, pair_hi, pair_lo, col_x, col_weight, grads, back, flat_out,
):
    flat_cols[...] = cols_ref[...].T
    for t in range(2):
        wrap_rows(flat_cols, t * CART, cols_p, t)
        wrap_rows(flat_cols, (2 + t) * CART, cols_c, t)

    extra = jnp.where(lax.broadcasted_iota(jnp.int32, (8, LANES), 0) == 0, 1.0, 0.0)
    nothing = jnp.zeros((8, LANES), f32)
    col_sq, col_xu = [], []
    for t in range(2):
        sq = nothing
        lanes_x = slice(t * LANES, (t + 1) * LANES)
        for d in separations:
            spans = spans_of(cols_p, (t,), d)
            inverse = lax.rsqrt(spans[0] * spans[0] + spans[1] * spans[1] + spans[2] * spans[2])
            at = rows_of(d)
            x = scale_ref[at, :] * inverse
            sq = sq + fold8(x * x)
            col_x[t, at, :] = x
            col_weight[t, at, :] = x * inverse * inverse
            if d == 0:
                x = jnp.concatenate([x, extra], 0)
                at = slice(LAST, ROWS)
            pair_hi[at, lanes_x], pair_lo[at, lanes_x] = halves(x)
        col_sq.append(jnp.sum(sq, axis=0, keepdims=True))

    count = 2 * LANES
    turned_hi, turned_lo = rowx_hi[...], rowx_lo[...]
    gram = (
        dot_nn(turned_hi, pair_hi[:, :count])
        + dot_nn(turned_hi, pair_lo[:, :count])
        + dot_nn(turned_lo, pair_hi[:, :count])
        + dot_nn(turned_lo, pair_lo[:, :count])
    )

    for t in range(2):
        xu = nothing
        lanes_u = slice((2 + t) * LANES, (3 + t) * LANES)
        for d in separations:
            spans = spans_of(cols_p, (t,), d)
            moves = spans_of(cols_c, (t,), d)
            at = rows_of(d)
            along = spans[0] * moves[0] + spans[1] * moves[1] + spans[2] * moves[2]
            u = -col_weight[t, at, :] * along
            xu = xu + fold8(col_x[t, at, :] * u)
            if d == 0:
                u = jnp.concatenate([u, nothing], 0)
                at = slice(LAST, ROWS)
            pair_hi[at, lanes_u], pair_lo[at, lanes_u] = halves(u)
        col_xu.append(jnp.sum(xu, axis=0, keepdims=True))

    cross = (
        dot_nn(turned_hi, pair_hi[:, count:])
        + dot_nn(turned_hi, pair_lo[:, count:])
        + dot_nn(turned_lo, pair_hi[:, count:])
    )
    sq_dist = row_sq[:, 0:1] + jnp.concatenate(col_sq, axis=1) - 2.0 * gram
    radius = jnp.sqrt(jnp.maximum(sq_dist, 0.0))
    envelope = outer_factor * jnp.exp(-decay_rate * radius)
    direct = envelope * (1.0 + decay_rate * radius)
    bent = (radial_factor * envelope) * (cross - jnp.concatenate(col_xu, axis=1))
    high, low = halves(jnp.concatenate([bent, direct], axis=1))
    for t in range(2):
        back[t] = jnp.zeros(back.shape[1:], f32)

    def multiply(first, end):
        at = slice((first - 1) * GROUP, ROWS if end == 9 else (end - 1) * GROUP)
        part_hi, part_lo = pair_hi[at, :], pair_lo[at, :]
        grads[at, :] = dot_nt(part_hi, high) + dot_nt(part_lo, high) + dot_nt(part_hi, low)

    def terms_of(t, d):
        at, lanes = rows_of(d), slice(t * LANES, (t + 1) * LANES)
        spans = spans_of(rows_w, (t,), d)
        inverse = lax.rsqrt(spans[0] * spans[0] + spans[1] * spans[1] + spans[2] * spans[2])
        x = scale_ref[at, :] * inverse
        bend = grads[PAIRS : PAIRS + 1, lanes]
        pull = (x * inverse * inverse) * (grads[at, lanes] - bend * x)
        return [pull * span for span in spans]

    def pull_back(t, first, end):
        here = [jnp.zeros((BLOCK, LANES), f32) for _ in range(3)]
        if end == 9:
            for k, term in enumerate(terms_of(t, 0)):
                back[t, k, 0:HALF, :] = term
                back[t, k, ATOMS - 1 : ATOMS, :] = -jnp.sum(term, axis=0, keepdims=True)
        for shift in range(first, end):
            there = [None] * 3
            for step in range(3):
                for k, term in enumerate(terms_of(t, shift + 8 * step)):
                    here[k] = here[k] + term
                    pieces = [term[8 * n : 8 * n + 8] for n in range(BLOCK // 8)]
                    if step == 0:
                        there[k] = pieces
                        continue
                    for n, piece in enumerate(pieces):
                        if step + n < len(there[k]):
                            there[k][step + n] = there[k][step + n] + piece
                        else:
                            there[k].append(piece)
            for k in range(3):
                total = jnp.concatenate(there[k], axis=0)
                at = slice(shift, shift + total.shape[0])
                back[t, k, at, :] = back[t, k, at, :] + total
        for k in range(3):
            back[t, k, 0:BLOCK, :] = back[t, k, 0:BLOCK, :] - here[k]

    multiply(*PARTS[0])
    for n, part in enumerate(PARTS):
        if n + 1 < len(PARTS):
            multiply(*PARTS[n + 1])
        for t in range(2):
            pull_back(t, *part)
    for t in range(2):
        for k in range(3):
            back[t, k, 0 : WRAP - ATOMS, :] = back[t, k, 0 : WRAP - ATOMS, :] + back[t, k, ATOMS:WRAP, :]
            base = t * CART + k * ATOMS
            flat_out[base : base + ATOMS, :] = back[t, k, 0:ATOMS, :]
    turned = flat_out[...].T
    for n, (at, size) in enumerate(place(flat_out.shape[1] // HALF_ROWS)):
        out_ref[pl.ds(at, size), :] = turned[n * size : (n + 1) * size, :]


def vmem(count):
    return [pl.BlockSpec(memory_space=pltpu.VMEM)] * count


def shape(*dims, kind=f32):
    return jax.ShapeDtypeStruct(dims, kind)


params = pltpu.CompilerParams(vmem_limit_bytes=16 * 1024 * 1024)


def row_terms(rows, atom_pairs, pair_scale):
    return pl.pallas_call(
        rows_kernel,
        out_shape=(
            shape(ROWS, LANES),
            shape(2, 3, WRAP, LANES),
            shape(2 * LANES, KDIM, kind=bf16),
            shape(2 * LANES, KDIM, kind=bf16),
            shape(2 * LANES, LANES),
        ),
        in_specs=vmem(3),
        out_specs=tuple(vmem(5)),
        scratch_shapes=[pltpu.VMEM((2 * CART, LANES), f32), pltpu.VMEM((2, ROWS, LANES), f32)],
        compiler_params=params,
        cost_estimate=pl.CostEstimate(
            flops=40_000_000, bytes_accessed=6_000_000, transcendentals=300_000
        ),
    )(rows, atom_pairs, pair_scale.reshape(1, -1))


def cols_apply(cols, terms, place):
    return pl.pallas_call(
        functools.partial(apply_kernel, place),
        out_shape=shape(LANES, 2 * CART),
        in_specs=vmem(1 + len(terms)),
        out_specs=vmem(1)[0],
        scratch_shapes=[
            pltpu.VMEM((4 * CART, LANES), f32),
            pltpu.VMEM((2, 3, WRAP, LANES), f32),
            pltpu.VMEM((2, 3, WRAP, LANES), f32),
            pltpu.VMEM((KDIM, 4 * LANES), bf16),
            pltpu.VMEM((KDIM, 4 * LANES), bf16),
            pltpu.VMEM((2, ROWS, LANES), f32),
            pltpu.VMEM((2, ROWS, LANES), f32),
            pltpu.VMEM((ROWS, 2 * LANES), f32),
            pltpu.VMEM((2, 3, WRAP, LANES), f32),
            pltpu.VMEM((2 * CART, LANES), f32),
        ],
        compiler_params=params,
        cost_estimate=pl.CostEstimate(
            flops=2_000_000_000, bytes_accessed=6_000_000, transcendentals=500_000
        ),
    )(cols, *terms)


def as_they_are(count):
    return [(0, count * HALF_ROWS)]


def tile_apply(rows, cols, atom_pairs, pair_scale, place=as_they_are):
    return cols_apply(cols, row_terms(rows, atom_pairs, pair_scale), place)


def side_by_side(value):
    half = value.shape[0] // 2
    return jnp.concatenate([value[:half], value[half:]], axis=1)


def exchange(value, axis):
    return lax.all_to_all(value, axis, split_axis=0, concat_axis=0, tiled=True)


def from_everyone(value, axis):
    copies = jnp.broadcast_to(value, (lax.axis_size(axis), *value.shape))
    return exchange(copies, axis).reshape(-1, value.shape[1])


def in_groups(value, axis, size):
    groups = [list(range(n, n + size)) for n in range(0, lax.axis_size(axis), size)]
    return lax.all_gather(value, axis, axis=0, tiled=True, axis_index_groups=groups)


def with_partners(value, axis, steps):
    count = lax.axis_size(axis)
    moved = [lax.ppermute(value, axis, [(n, n ^ step) for n in range(count)]) for step in steps]
    return jnp.concatenate([value, *moved], axis=0)


def row_gather(value, axis):
    return with_partners(in_groups(value, axis, 4), axis, (4, 8, 12))


def owners_place(count):
    own = 4 * (lax.axis_index("row") // 4)
    size = 4 * HALF_ROWS
    return [(pl.multiple_of((own ^ step) * HALF_ROWS, size), size) for step in range(0, count, 4)]


def on_device(positions, coefficients, atom_pairs, pair_scale):
    packed = jnp.concatenate([side_by_side(positions), side_by_side(coefficients)], axis=1)
    cols = from_everyone(packed, "col")
    rows = row_gather(packed[:, : 2 * CART], "row")
    partial = tile_apply(rows, cols, atom_pairs, pair_scale, owners_place)
    arrived = exchange(partial.reshape(lax.axis_size("row"), -1, 2 * CART), "row")
    total = arrived.sum(axis=0)
    return jnp.concatenate([total[:, :CART], total[:, CART:]], axis=0)


def solution(mesh):
    in_specs = (P(("row", "col"), None), P(("row", "col"), None), P(), P())
    out_specs = P(("row", "col"), None)
    return jax.shard_map(
        on_device, mesh=mesh, in_specs=in_specs, out_specs=out_specs, check_vma=False
    )
```

```python
import functools
import math

import jax
import jax.numpy as jnp
from jax import lax
from jax.experimental import pallas as pl
from jax.experimental.pallas import tpu as pltpu
from jax.sharding import PartitionSpec as P

ATOMS = 49
HALF = 24
BLOCK = 48
LAST = HALF * BLOCK
PAIRS = LAST + HALF
ROWS = PAIRS + 8
KDIM = ROWS
HALF_ROWS = 8
WRAP = 72
CART = 3 * ATOMS
LANES = 128

length_scale = 2.0
decay_rate = math.sqrt(5.0) / length_scale
outer_factor = decay_rate * decay_rate / 3.0
radial_factor = decay_rate * decay_rate
f32 = jnp.float32
bf16 = jnp.bfloat16


def halves(value):
    high = value.astype(bf16)
    return high, (value - high.astype(f32)).astype(bf16)


def dot_nt(a, b):
    return lax.dot_general(a, b, (((1,), (1,)), ((), ())), preferred_element_type=f32)


def dot_nn(a, b):
    return lax.dot_general(a, b, (((1,), (0,)), ((), ())), preferred_element_type=f32)


def spread_scale(pairs_ref, scale_ref, out_ref):
    low, high = pairs_ref[0:1, :], pairs_ref[1:2, :]
    apart = high - low
    near = apart <= HALF
    shift = jnp.where(near, apart, ATOMS - apart) - 1
    start = jnp.where(near, low, high)
    count = low.shape[1]
    atom_ids = lax.broadcasted_iota(jnp.int32, (64, count), 0)
    shift_ids = lax.broadcasted_iota(jnp.int32, (32, count), 0)
    at_atom = jnp.where(atom_ids == start, 1.0, 0.0).astype(bf16)
    scaled = jnp.where(shift_ids == shift, scale_ref[...], 0.0)
    top = scaled.astype(bf16)
    rest = scaled - top.astype(f32)
    middle = rest.astype(bf16)
    bottom = (rest - middle.astype(f32)).astype(bf16)
    table = dot_nt(at_atom, top) + dot_nt(at_atom, middle) + dot_nt(at_atom, bottom)
    for d in range(HALF):
        out_ref[rows_of(d + 1), :] = jnp.broadcast_to(
            table[0:BLOCK, d : d + 1], (BLOCK, LANES)
        )
    last = jnp.where(start == ATOMS - 1, scaled, 0.0)
    last = jnp.sum(last[0:HALF], axis=1, keepdims=True)
    out_ref[LAST:PAIRS, :] = jnp.broadcast_to(last, (HALF, LANES))


def wrap_rows(flat_ref, start, wrapped_ref, *at):
    for k in range(3):
        base = start + k * ATOMS
        wrapped_ref[(*at, k, slice(0, ATOMS), slice(None))] = flat_ref[base : base + ATOMS, :]
        wrapped_ref[(*at, k, slice(ATOMS, WRAP), slice(None))] = flat_ref[
            base : base + WRAP - ATOMS, :
        ]


def spans_of(wrapped_ref, at, d):
    if d == 0:
        here, there = slice(ATOMS - 1, ATOMS), slice(0, HALF)
    else:
        here, there = slice(0, BLOCK), slice(d, d + BLOCK)
    return [
        wrapped_ref[(*at, k, here, slice(None))] - wrapped_ref[(*at, k, there, slice(None))]
        for k in range(3)
    ]


def rows_of(d):
    if d == 0:
        return slice(LAST, PAIRS)
    place = 3 * ((d - 1) % 8) + (d - 1) // 8
    return slice(place * BLOCK, (place + 1) * BLOCK)


GROUP = 3 * BLOCK
PARTS = ((7, 9), (1, 3), (3, 5), (5, 7))
separations = (*range(1, HALF + 1), 0)


def fold8(value):
    total = value[0:8]
    for n in range(1, value.shape[0] // 8):
        total = total + value[8 * n : 8 * n + 8]
    return total


def rows_kernel(
    rows_ref, pairs_ref, pair_scale_ref,
    scale_ref, rows_w, rowx_hi, rowx_lo, row_sq,
    flat_rows, row_x,
):
    spread_scale(pairs_ref, pair_scale_ref, scale_ref)
    flat_rows[...] = rows_ref[...].T
    for t in range(2):
        wrap_rows(flat_rows, t * CART, rows_w, t)
    nothing = jnp.zeros((8, LANES), f32)
    for t in range(2):
        for d in separations:
            at = rows_of(d)
            spans = spans_of(rows_w, (t,), d)
            inverse = lax.rsqrt(spans[0] * spans[0] + spans[1] * spans[1] + spans[2] * spans[2])
            x = scale_ref[at, :] * inverse
            row_x[t, at, :] = x
        row_x[t, PAIRS:ROWS, :] = nothing
        sq = 0.0
        for start in range(0, ROWS, LANES):
            stop = min(start + LANES, ROWS)
            turned = row_x[t, start:stop, :].T
            high = turned.astype(bf16)
            rest = turned - high.astype(f32)
            at = slice(t * LANES, (t + 1) * LANES)
            rowx_hi[at, start:stop] = high
            rowx_lo[at, start:stop] = rest.astype(bf16)
            sq = sq + jnp.sum(turned * turned, axis=1, keepdims=True)
        row_sq[t * LANES : (t + 1) * LANES, :] = jnp.broadcast_to(sq, (LANES, LANES))


def apply_kernel(
    place, cols_ref, scale_ref, rows_w, rowx_hi, rowx_lo, row_sq, out_ref,
    flat_cols, cols_p, cols_c, pair_hi, pair_lo, col_x, col_weight, grads, back, flat_out,
):
    flat_cols[...] = cols_ref[...].T
    for t in range(2):
        wrap_rows(flat_cols, t * CART, cols_p, t)
        wrap_rows(flat_cols, (2 + t) * CART, cols_c, t)

    extra = jnp.where(lax.broadcasted_iota(jnp.int32, (8, LANES), 0) == 0, 1.0, 0.0)
    nothing = jnp.zeros((8, LANES), f32)
    col_sq, col_xu = [], []
    for t in range(2):
        sq = nothing
        lanes_x = slice(t * LANES, (t + 1) * LANES)
        for d in separations:
            spans = spans_of(cols_p, (t,), d)
            inverse = lax.rsqrt(spans[0] * spans[0] + spans[1] * spans[1] + spans[2] * spans[2])
            at = rows_of(d)
            x = scale_ref[at, :] * inverse
            sq = sq + fold8(x * x)
            col_x[t, at, :] = x
            col_weight[t, at, :] = x * inverse * inverse
            if d == 0:
                x = jnp.concatenate([x, extra], 0)
                at = slice(LAST, ROWS)
            pair_hi[at, lanes_x], pair_lo[at, lanes_x] = halves(x)
        col_sq.append(jnp.sum(sq, axis=0, keepdims=True))

    count = 2 * LANES
    turned_hi, turned_lo = rowx_hi[...], rowx_lo[...]
    gram = (
        dot_nn(turned_hi, pair_hi[:, :count])
        + dot_nn(turned_hi, pair_lo[:, :count])
        + dot_nn(turned_lo, pair_hi[:, :count])
        + dot_nn(turned_lo, pair_lo[:, :count])
    )

    for t in range(2):
        xu = nothing
        lanes_u = slice((2 + t) * LANES, (3 + t) * LANES)
        for d in separations:
            spans = spans_of(cols_p, (t,), d)
            moves = spans_of(cols_c, (t,), d)
            at = rows_of(d)
            along = spans[0] * moves[0] + spans[1] * moves[1] + spans[2] * moves[2]
            u = -col_weight[t, at, :] * along
            xu = xu + fold8(col_x[t, at, :] * u)
            if d == 0:
                u = jnp.concatenate([u, nothing], 0)
                at = slice(LAST, ROWS)
            pair_hi[at, lanes_u], pair_lo[at, lanes_u] = halves(u)
        col_xu.append(jnp.sum(xu, axis=0, keepdims=True))

    cross = (
        dot_nn(turned_hi, pair_hi[:, count:])
        + dot_nn(turned_hi, pair_lo[:, count:])
        + dot_nn(turned_lo, pair_hi[:, count:])
    )
    sq_dist = row_sq[:, 0:1] + jnp.concatenate(col_sq, axis=1) - 2.0 * gram
    radius = jnp.sqrt(jnp.maximum(sq_dist, 0.0))
    envelope = outer_factor * jnp.exp(-decay_rate * radius)
    direct = envelope * (1.0 + decay_rate * radius)
    bent = (radial_factor * envelope) * (cross - jnp.concatenate(col_xu, axis=1))
    high, low = halves(jnp.concatenate([bent, direct], axis=1))
    for t in range(2):
        back[t] = jnp.zeros(back.shape[1:], f32)

    def multiply(first, end):
        at = slice((first - 1) * GROUP, ROWS if end == 9 else (end - 1) * GROUP)
        part_hi, part_lo = pair_hi[at, :], pair_lo[at, :]
        grads[at, :] = dot_nt(part_hi, high) + dot_nt(part_lo, high) + dot_nt(part_hi, low)

    def terms_of(t, d):
        at, lanes = rows_of(d), slice(t * LANES, (t + 1) * LANES)
        spans = spans_of(rows_w, (t,), d)
        inverse = lax.rsqrt(spans[0] * spans[0] + spans[1] * spans[1] + spans[2] * spans[2])
        x = scale_ref[at, :] * inverse
        bend = grads[PAIRS : PAIRS + 1, lanes]
        pull = (x * inverse * inverse) * (grads[at, lanes] - bend * x)
        return [pull * span for span in spans]

    def pull_back(t, first, end):
        here = [jnp.zeros((BLOCK, LANES), f32) for _ in range(3)]
        if end == 9:
            for k, term in enumerate(terms_of(t, 0)):
                back[t, k, 0:HALF, :] = term
                back[t, k, ATOMS - 1 : ATOMS, :] = -jnp.sum(term, axis=0, keepdims=True)
        for shift in range(first, end):
            there = [None] * 3
            for step in range(3):
                for k, term in enumerate(terms_of(t, shift + 8 * step)):
                    here[k] = here[k] + term
                    pieces = [term[8 * n : 8 * n + 8] for n in range(BLOCK // 8)]
                    if step == 0:
                        there[k] = pieces
                        continue
                    for n, piece in enumerate(pieces):
                        if step + n < len(there[k]):
                            there[k][step + n] = there[k][step + n] + piece
                        else:
                            there[k].append(piece)
            for k in range(3):
                total = jnp.concatenate(there[k], axis=0)
                at = slice(shift, shift + total.shape[0])
                back[t, k, at, :] = back[t, k, at, :] + total
        for k in range(3):
            back[t, k, 0:BLOCK, :] = back[t, k, 0:BLOCK, :] - here[k]

    multiply(*PARTS[0])
    for n, part in enumerate(PARTS):
        if n + 1 < len(PARTS):
            multiply(*PARTS[n + 1])
        for t in range(2):
            pull_back(t, *part)
    for t in range(2):
        for k in range(3):
            back[t, k, 0 : WRAP - ATOMS, :] = back[t, k, 0 : WRAP - ATOMS, :] + back[t, k, ATOMS:WRAP, :]
            base = t * CART + k * ATOMS
            flat_out[base : base + ATOMS, :] = back[t, k, 0:ATOMS, :]
    turned = flat_out[...].T
    for n, (at, size) in enumerate(place(flat_out.shape[1] // HALF_ROWS)):
        out_ref[pl.ds(at, size), :] = turned[n * size : (n + 1) * size, :]


def vmem(count):
    return [pl.BlockSpec(memory_space=pltpu.VMEM)] * count


def shape(*dims, kind=f32):
    return jax.ShapeDtypeStruct(dims, kind)


params = pltpu.CompilerParams(vmem_limit_bytes=16 * 1024 * 1024)


def row_terms(rows, atom_pairs, pair_scale):
    return pl.pallas_call(
        rows_kernel,
        out_shape=(
            shape(ROWS, LANES),
            shape(2, 3, WRAP, LANES),
            shape(2 * LANES, KDIM, kind=bf16),
            shape(2 * LANES, KDIM, kind=bf16),
            shape(2 * LANES, LANES),
        ),
        in_specs=vmem(3),
        out_specs=tuple(vmem(5)),
        scratch_shapes=[pltpu.VMEM((2 * CART, LANES), f32), pltpu.VMEM((2, ROWS, LANES), f32)],
        compiler_params=params,
        cost_estimate=pl.CostEstimate(
            flops=40_000_000, bytes_accessed=6_000_000, transcendentals=300_000
        ),
    )(rows, atom_pairs, pair_scale.reshape(1, -1))


def cols_apply(cols, terms, place):
    return pl.pallas_call(
        functools.partial(apply_kernel, place),
        out_shape=shape(LANES, 2 * CART),
        in_specs=vmem(1 + len(terms)),
        out_specs=vmem(1)[0],
        scratch_shapes=[
            pltpu.VMEM((4 * CART, LANES), f32),
            pltpu.VMEM((2, 3, WRAP, LANES), f32),
            pltpu.VMEM((2, 3, WRAP, LANES), f32),
            pltpu.VMEM((KDIM, 4 * LANES), bf16),
            pltpu.VMEM((KDIM, 4 * LANES), bf16),
            pltpu.VMEM((2, ROWS, LANES), f32),
            pltpu.VMEM((2, ROWS, LANES), f32),
            pltpu.VMEM((ROWS, 2 * LANES), f32),
            pltpu.VMEM((2, 3, WRAP, LANES), f32),
            pltpu.VMEM((2 * CART, LANES), f32),
        ],
        compiler_params=params,
        cost_estimate=pl.CostEstimate(
            flops=2_000_000_000, bytes_accessed=6_000_000, transcendentals=500_000
        ),
    )(cols, *terms)


def as_they_are(count):
    return [(0, count * HALF_ROWS)]


def tile_apply(rows, cols, atom_pairs, pair_scale, place=as_they_are):
    return cols_apply(cols, row_terms(rows, atom_pairs, pair_scale), place)


def side_by_side(value):
    half = value.shape[0] // 2
    return jnp.concatenate([value[:half], value[half:]], axis=1)


def exchange(value, axis):
    return lax.all_to_all(value, axis, split_axis=0, concat_axis=0, tiled=True)


def from_everyone(value, axis):
    copies = jnp.broadcast_to(value, (lax.axis_size(axis), *value.shape))
    return exchange(copies, axis).reshape(-1, value.shape[1])


def in_groups(value, axis, size):
    groups = [list(range(n, n + size)) for n in range(0, lax.axis_size(axis), size)]
    return lax.all_gather(value, axis, axis=0, tiled=True, axis_index_groups=groups)


def with_partners(value, axis, steps):
    count = lax.axis_size(axis)
    moved = [lax.ppermute(value, axis, [(n, n ^ step) for n in range(count)]) for step in steps]
    return jnp.concatenate([value, *moved], axis=0)


def row_gather(value, axis):
    return in_groups(with_partners(value, axis, (4, 8, 12)), axis, 4)


def owners_place(count):
    own = lax.axis_index("row")
    first = 4 * (own // 4)
    numbers = [(first ^ step) + n for n in range(4) for step in (0, 4, 8, 12)]
    return [(pl.multiple_of(at * HALF_ROWS, HALF_ROWS), HALF_ROWS) for at in numbers]


def on_device(positions, coefficients, atom_pairs, pair_scale):
    packed = jnp.concatenate([side_by_side(positions), side_by_side(coefficients)], axis=1)
    cols = from_everyone(packed, "col")
    rows = row_gather(packed[:, : 2 * CART], "row")
    partial = tile_apply(rows, cols, atom_pairs, pair_scale, owners_place)
    arrived = exchange(partial.reshape(lax.axis_size("row"), -1, 2 * CART), "row")
    total = arrived.sum(axis=0)
    return jnp.concatenate([total[:, :CART], total[:, CART:]], axis=0)


def solution(mesh):
    in_specs = (P(("row", "col"), None), P(("row", "col"), None), P(), P())
    out_specs = P(("row", "col"), None)
    return jax.shard_map(
        on_device, mesh=mesh, in_specs=in_specs, out_specs=out_specs, check_vma=False
    )
```

```python
import functools
import math

import jax
import jax.numpy as jnp
from jax import lax
from jax.experimental import pallas as pl
from jax.experimental.pallas import tpu as pltpu
from jax.sharding import PartitionSpec as P

ATOMS = 49
HALF = 24
BLOCK = 48
LAST = HALF * BLOCK
PAIRS = LAST + HALF
ROWS = PAIRS + 8
KDIM = ROWS
HALF_ROWS = 8
WRAP = 72
CART = 3 * ATOMS
LANES = 128

length_scale = 2.0
decay_rate = math.sqrt(5.0) / length_scale
outer_factor = decay_rate * decay_rate / 3.0
radial_factor = decay_rate * decay_rate
f32 = jnp.float32
bf16 = jnp.bfloat16


def halves(value):
    high = value.astype(bf16)
    return high, (value - high.astype(f32)).astype(bf16)


def dot_nt(a, b):
    return lax.dot_general(a, b, (((1,), (1,)), ((), ())), preferred_element_type=f32)


def dot_nn(a, b):
    return lax.dot_general(a, b, (((1,), (0,)), ((), ())), preferred_element_type=f32)


def spread_scale(pairs_ref, scale_ref, out_ref):
    low, high = pairs_ref[0:1, :], pairs_ref[1:2, :]
    apart = high - low
    near = apart <= HALF
    shift = jnp.where(near, apart, ATOMS - apart) - 1
    start = jnp.where(near, low, high)
    count = low.shape[1]
    atom_ids = lax.broadcasted_iota(jnp.int32, (64, count), 0)
    shift_ids = lax.broadcasted_iota(jnp.int32, (32, count), 0)
    at_atom = jnp.where(atom_ids == start, 1.0, 0.0).astype(bf16)
    scaled = jnp.where(shift_ids == shift, scale_ref[...], 0.0)
    top = scaled.astype(bf16)
    rest = scaled - top.astype(f32)
    middle = rest.astype(bf16)
    bottom = (rest - middle.astype(f32)).astype(bf16)
    table = dot_nt(at_atom, top) + dot_nt(at_atom, middle) + dot_nt(at_atom, bottom)
    for d in range(HALF):
        out_ref[rows_of(d + 1), :] = jnp.broadcast_to(
            table[0:BLOCK, d : d + 1], (BLOCK, LANES)
        )
    last = jnp.where(start == ATOMS - 1, scaled, 0.0)
    last = jnp.sum(last[0:HALF], axis=1, keepdims=True)
    out_ref[LAST:PAIRS, :] = jnp.broadcast_to(last, (HALF, LANES))


def wrap_rows(flat_ref, start, wrapped_ref, *at):
    for k in range(3):
        base = start + k * ATOMS
        wrapped_ref[(*at, k, slice(0, ATOMS), slice(None))] = flat_ref[base : base + ATOMS, :]
        wrapped_ref[(*at, k, slice(ATOMS, WRAP), slice(None))] = flat_ref[
            base : base + WRAP - ATOMS, :
        ]


def spans_of(wrapped_ref, at, d):
    if d == 0:
        here, there = slice(ATOMS - 1, ATOMS), slice(0, HALF)
    else:
        here, there = slice(0, BLOCK), slice(d, d + BLOCK)
    return [
        wrapped_ref[(*at, k, here, slice(None))] - wrapped_ref[(*at, k, there, slice(None))]
        for k in range(3)
    ]


def rows_of(d):
    if d == 0:
        return slice(LAST, PAIRS)
    place = 3 * ((d - 1) % 8) + (d - 1) // 8
    return slice(place * BLOCK, (place + 1) * BLOCK)


GROUP = 3 * BLOCK
PARTS = ((7, 9), (1, 3), (3, 5), (5, 7))
separations = (*range(1, HALF + 1), 0)


def fold8(value):
    total = value[0:8]
    for n in range(1, value.shape[0] // 8):
        total = total + value[8 * n : 8 * n + 8]
    return total


def rows_kernel(
    rows_ref, pairs_ref, pair_scale_ref,
    scale_ref, rows_w, rowx_hi, rowx_lo, row_sq,
    flat_rows, row_x,
):
    spread_scale(pairs_ref, pair_scale_ref, scale_ref)
    flat_rows[...] = rows_ref[...].T
    for t in range(2):
        wrap_rows(flat_rows, t * CART, rows_w, t)
    nothing = jnp.zeros((8, LANES), f32)
    for t in range(2):
        for d in separations:
            at = rows_of(d)
            spans = spans_of(rows_w, (t,), d)
            inverse = lax.rsqrt(spans[0] * spans[0] + spans[1] * spans[1] + spans[2] * spans[2])
            x = scale_ref[at, :] * inverse
            row_x[t, at, :] = x
        row_x[t, PAIRS:ROWS, :] = nothing
        sq = 0.0
        for start in range(0, ROWS, LANES):
            stop = min(start + LANES, ROWS)
            turned = row_x[t, start:stop, :].T
            high = turned.astype(bf16)
            rest = turned - high.astype(f32)
            at = slice(t * LANES, (t + 1) * LANES)
            rowx_hi[at, start:stop] = high
            rowx_lo[at, start:stop] = rest.astype(bf16)
            sq = sq + jnp.sum(turned * turned, axis=1, keepdims=True)
        row_sq[t * LANES : (t + 1) * LANES, :] = jnp.broadcast_to(sq, (LANES, LANES))


def apply_kernel(
    place, cols_ref, scale_ref, rows_w, rowx_hi, rowx_lo, row_sq, out_ref,
    flat_cols, cols_p, cols_c, pair_hi, pair_lo, col_x, col_weight, grads, back, flat_out,
):
    flat_cols[...] = cols_ref[...].T
    for t in range(2):
        wrap_rows(flat_cols, t * CART, cols_p, t)
        wrap_rows(flat_cols, (2 + t) * CART, cols_c, t)

    extra = jnp.where(lax.broadcasted_iota(jnp.int32, (8, LANES), 0) == 0, 1.0, 0.0)
    nothing = jnp.zeros((8, LANES), f32)
    col_sq, col_xu = [], []
    for t in range(2):
        sq = nothing
        lanes_x = slice(t * LANES, (t + 1) * LANES)
        for d in separations:
            spans = spans_of(cols_p, (t,), d)
            inverse = lax.rsqrt(spans[0] * spans[0] + spans[1] * spans[1] + spans[2] * spans[2])
            at = rows_of(d)
            x = scale_ref[at, :] * inverse
            sq = sq + fold8(x * x)
            col_x[t, at, :] = x
            col_weight[t, at, :] = x * inverse * inverse
            if d == 0:
                x = jnp.concatenate([x, extra], 0)
                at = slice(LAST, ROWS)
            pair_hi[at, lanes_x], pair_lo[at, lanes_x] = halves(x)
        col_sq.append(jnp.sum(sq, axis=0, keepdims=True))

    count = 2 * LANES
    turned = jnp.concatenate([rowx_hi[...], rowx_lo[...]], axis=0)
    with_high, with_low = dot_nn(turned, pair_hi[:, :count]), dot_nn(turned, pair_lo[:, :count])
    gram = (with_high[:count] + with_high[count:]) + (with_low[:count] + with_low[count:])

    for t in range(2):
        xu = nothing
        lanes_u = slice((2 + t) * LANES, (3 + t) * LANES)
        for d in separations:
            spans = spans_of(cols_p, (t,), d)
            moves = spans_of(cols_c, (t,), d)
            at = rows_of(d)
            along = spans[0] * moves[0] + spans[1] * moves[1] + spans[2] * moves[2]
            u = -col_weight[t, at, :] * along
            xu = xu + fold8(col_x[t, at, :] * u)
            if d == 0:
                u = jnp.concatenate([u, nothing], 0)
                at = slice(LAST, ROWS)
            pair_hi[at, lanes_u], pair_lo[at, lanes_u] = halves(u)
        col_xu.append(jnp.sum(xu, axis=0, keepdims=True))

    with_high = dot_nn(turned, pair_hi[:, count:])
    cross = with_high[:count] + with_high[count:] + dot_nn(rowx_hi[...], pair_lo[:, count:])
    sq_dist = row_sq[:, 0:1] + jnp.concatenate(col_sq, axis=1) - 2.0 * gram
    radius = jnp.sqrt(jnp.maximum(sq_dist, 0.0))
    envelope = outer_factor * jnp.exp(-decay_rate * radius)
    direct = envelope * (1.0 + decay_rate * radius)
    bent = (radial_factor * envelope) * (cross - jnp.concatenate(col_xu, axis=1))
    high, low = halves(jnp.concatenate([bent, direct], axis=1))
    for t in range(2):
        back[t] = jnp.zeros(back.shape[1:], f32)

    def multiply(first, end):
        at = slice((first - 1) * GROUP, ROWS if end == 9 else (end - 1) * GROUP)
        part_hi, part_lo = pair_hi[at, :], pair_lo[at, :]
        both = dot_nt(jnp.concatenate([part_hi, part_lo], axis=0), high)
        size = part_hi.shape[0]
        grads[at, :] = both[:size] + both[size:] + dot_nt(part_hi, low)

    def terms_of(t, d):
        at, lanes = rows_of(d), slice(t * LANES, (t + 1) * LANES)
        spans = spans_of(rows_w, (t,), d)
        inverse = lax.rsqrt(spans[0] * spans[0] + spans[1] * spans[1] + spans[2] * spans[2])
        x = scale_ref[at, :] * inverse
        bend = grads[PAIRS : PAIRS + 1, lanes]
        pull = (x * inverse * inverse) * (grads[at, lanes] - bend * x)
        return [pull * span for span in spans]

    def pull_back(t, first, end):
        here = [jnp.zeros((BLOCK, LANES), f32) for _ in range(3)]
        if end == 9:
            for k, term in enumerate(terms_of(t, 0)):
                back[t, k, 0:HALF, :] = term
                back[t, k, ATOMS - 1 : ATOMS, :] = -jnp.sum(term, axis=0, keepdims=True)
        for shift in range(first, end):
            there = [None] * 3
            for step in range(3):
                for k, term in enumerate(terms_of(t, shift + 8 * step)):
                    here[k] = here[k] + term
                    pieces = [term[8 * n : 8 * n + 8] for n in range(BLOCK // 8)]
                    if step == 0:
                        there[k] = pieces
                        continue
                    for n, piece in enumerate(pieces):
                        if step + n < len(there[k]):
                            there[k][step + n] = there[k][step + n] + piece
                        else:
                            there[k].append(piece)
            for k in range(3):
                total = jnp.concatenate(there[k], axis=0)
                at = slice(shift, shift + total.shape[0])
                back[t, k, at, :] = back[t, k, at, :] + total
        for k in range(3):
            back[t, k, 0:BLOCK, :] = back[t, k, 0:BLOCK, :] - here[k]

    multiply(*PARTS[0])
    for n, part in enumerate(PARTS):
        if n + 1 < len(PARTS):
            multiply(*PARTS[n + 1])
        for t in range(2):
            pull_back(t, *part)
    for t in range(2):
        for k in range(3):
            back[t, k, 0 : WRAP - ATOMS, :] = back[t, k, 0 : WRAP - ATOMS, :] + back[t, k, ATOMS:WRAP, :]
            base = t * CART + k * ATOMS
            flat_out[base : base + ATOMS, :] = back[t, k, 0:ATOMS, :]
    turned = flat_out[...].T
    for n, (at, size) in enumerate(place(flat_out.shape[1] // HALF_ROWS)):
        out_ref[pl.ds(at, size), :] = turned[n * size : (n + 1) * size, :]


def vmem(count):
    return [pl.BlockSpec(memory_space=pltpu.VMEM)] * count


def shape(*dims, kind=f32):
    return jax.ShapeDtypeStruct(dims, kind)


params = pltpu.CompilerParams(vmem_limit_bytes=16 * 1024 * 1024)


def row_terms(rows, atom_pairs, pair_scale):
    return pl.pallas_call(
        rows_kernel,
        out_shape=(
            shape(ROWS, LANES),
            shape(2, 3, WRAP, LANES),
            shape(2 * LANES, KDIM, kind=bf16),
            shape(2 * LANES, KDIM, kind=bf16),
            shape(2 * LANES, LANES),
        ),
        in_specs=vmem(3),
        out_specs=tuple(vmem(5)),
        scratch_shapes=[pltpu.VMEM((2 * CART, LANES), f32), pltpu.VMEM((2, ROWS, LANES), f32)],
        compiler_params=params,
        cost_estimate=pl.CostEstimate(
            flops=40_000_000, bytes_accessed=6_000_000, transcendentals=300_000
        ),
    )(rows, atom_pairs, pair_scale.reshape(1, -1))


def cols_apply(cols, terms, place):
    return pl.pallas_call(
        functools.partial(apply_kernel, place),
        out_shape=shape(LANES, 2 * CART),
        in_specs=vmem(1 + len(terms)),
        out_specs=vmem(1)[0],
        scratch_shapes=[
            pltpu.VMEM((4 * CART, LANES), f32),
            pltpu.VMEM((2, 3, WRAP, LANES), f32),
            pltpu.VMEM((2, 3, WRAP, LANES), f32),
            pltpu.VMEM((KDIM, 4 * LANES), bf16),
            pltpu.VMEM((KDIM, 4 * LANES), bf16),
            pltpu.VMEM((2, ROWS, LANES), f32),
            pltpu.VMEM((2, ROWS, LANES), f32),
            pltpu.VMEM((ROWS, 2 * LANES), f32),
            pltpu.VMEM((2, 3, WRAP, LANES), f32),
            pltpu.VMEM((2 * CART, LANES), f32),
        ],
        compiler_params=params,
        cost_estimate=pl.CostEstimate(
            flops=2_000_000_000, bytes_accessed=6_000_000, transcendentals=500_000
        ),
    )(cols, *terms)


def as_they_are(count):
    return [(0, count * HALF_ROWS)]


def tile_apply(rows, cols, atom_pairs, pair_scale, place=as_they_are):
    return cols_apply(cols, row_terms(rows, atom_pairs, pair_scale), place)


def side_by_side(value):
    half = value.shape[0] // 2
    return jnp.concatenate([value[:half], value[half:]], axis=1)


def exchange(value, axis):
    return lax.all_to_all(value, axis, split_axis=0, concat_axis=0, tiled=True)


def from_everyone(value, axis):
    copies = jnp.broadcast_to(value, (lax.axis_size(axis), *value.shape))
    return exchange(copies, axis).reshape(-1, value.shape[1])


def in_groups(value, axis, size):
    groups = [list(range(n, n + size)) for n in range(0, lax.axis_size(axis), size)]
    return lax.all_gather(value, axis, axis=0, tiled=True, axis_index_groups=groups)


def with_partners(value, axis, steps):
    count = lax.axis_size(axis)
    moved = [lax.ppermute(value, axis, [(n, n ^ step) for n in range(count)]) for step in steps]
    return jnp.concatenate([value, *moved], axis=0)


def row_gather(value, axis):
    return in_groups(with_partners(value, axis, (4, 8, 12)), axis, 4)


def owners_place(count):
    own = lax.axis_index("row")
    first = 4 * (own // 4)
    numbers = [(first ^ step) + n for n in range(4) for step in (0, 4, 8, 12)]
    return [(pl.multiple_of(at * HALF_ROWS, HALF_ROWS), HALF_ROWS) for at in numbers]


def on_device(positions, coefficients, atom_pairs, pair_scale):
    packed = jnp.concatenate([side_by_side(positions), side_by_side(coefficients)], axis=1)
    cols = from_everyone(packed, "col")
    rows = row_gather(packed[:, : 2 * CART], "row")
    partial = tile_apply(rows, cols, atom_pairs, pair_scale, owners_place)
    arrived = exchange(partial.reshape(lax.axis_size("row"), -1, 2 * CART), "row")
    total = arrived.sum(axis=0)
    return jnp.concatenate([total[:, :CART], total[:, CART:]], axis=0)


def solution(mesh):
    in_specs = (P(("row", "col"), None), P(("row", "col"), None), P(), P())
    out_specs = P(("row", "col"), None)
    return jax.shard_map(
        on_device, mesh=mesh, in_specs=in_specs, out_specs=out_specs, check_vma=False
    )
```

```python
import functools
import math

import jax
import jax.numpy as jnp
from jax import lax
from jax.experimental import pallas as pl
from jax.experimental.pallas import tpu as pltpu
from jax.sharding import PartitionSpec as P

ATOMS = 49
HALF = 24
BLOCK = 48
LAST = HALF * BLOCK
PAIRS = LAST + HALF
ROWS = PAIRS + 8
KDIM = ROWS
HALF_ROWS = 8
WRAP = 72
CART = 3 * ATOMS
LANES = 128

length_scale = 2.0
decay_rate = math.sqrt(5.0) / length_scale
outer_factor = decay_rate * decay_rate / 3.0
radial_factor = decay_rate * decay_rate
f32 = jnp.float32
bf16 = jnp.bfloat16


def halves(value):
    high = value.astype(bf16)
    return high, (value - high.astype(f32)).astype(bf16)


def dot_nt(a, b):
    return lax.dot_general(a, b, (((1,), (1,)), ((), ())), preferred_element_type=f32)


def dot_nn(a, b):
    return lax.dot_general(a, b, (((1,), (0,)), ((), ())), preferred_element_type=f32)


def spread_scale(pairs_ref, scale_ref, out_ref):
    low, high = pairs_ref[0:1, :], pairs_ref[1:2, :]
    apart = high - low
    near = apart <= HALF
    shift = jnp.where(near, apart, ATOMS - apart) - 1
    start = jnp.where(near, low, high)
    count = low.shape[1]
    atom_ids = lax.broadcasted_iota(jnp.int32, (64, count), 0)
    shift_ids = lax.broadcasted_iota(jnp.int32, (32, count), 0)
    at_atom = jnp.where(atom_ids == start, 1.0, 0.0).astype(bf16)
    scaled = jnp.where(shift_ids == shift, scale_ref[...], 0.0)
    top = scaled.astype(bf16)
    rest = scaled - top.astype(f32)
    middle = rest.astype(bf16)
    bottom = (rest - middle.astype(f32)).astype(bf16)
    table = dot_nt(at_atom, top) + dot_nt(at_atom, middle) + dot_nt(at_atom, bottom)
    for d in range(HALF):
        out_ref[rows_of(d + 1), :] = jnp.broadcast_to(
            table[0:BLOCK, d : d + 1], (BLOCK, LANES)
        )
    last = jnp.where(start == ATOMS - 1, scaled, 0.0)
    last = jnp.sum(last[0:HALF], axis=1, keepdims=True)
    out_ref[LAST:PAIRS, :] = jnp.broadcast_to(last, (HALF, LANES))


def wrap_rows(flat_ref, start, wrapped_ref, *at):
    for k in range(3):
        base = start + k * ATOMS
        wrapped_ref[(*at, k, slice(0, ATOMS), slice(None))] = flat_ref[base : base + ATOMS, :]
        wrapped_ref[(*at, k, slice(ATOMS, WRAP), slice(None))] = flat_ref[
            base : base + WRAP - ATOMS, :
        ]


def spans_of(wrapped_ref, at, d):
    if d == 0:
        here, there = slice(ATOMS - 1, ATOMS), slice(0, HALF)
    else:
        here, there = slice(0, BLOCK), slice(d, d + BLOCK)
    return [
        wrapped_ref[(*at, k, here, slice(None))] - wrapped_ref[(*at, k, there, slice(None))]
        for k in range(3)
    ]


def rows_of(d):
    if d == 0:
        return slice(LAST, PAIRS)
    place = 3 * ((d - 1) % 8) + (d - 1) // 8
    return slice(place * BLOCK, (place + 1) * BLOCK)


GROUP = 3 * BLOCK
PARTS = ((7, 9), (1, 3), (3, 5), (5, 7))
separations = (*range(1, HALF + 1), 0)


def fold8(value):
    total = value[0:8]
    for n in range(1, value.shape[0] // 8):
        total = total + value[8 * n : 8 * n + 8]
    return total


def rows_kernel(
    rows_ref, scale_ref,
    rows_w, rowx_hi, rowx_lo, row_sq,
    flat_rows, row_x,
):
    flat_rows[...] = rows_ref[...].T
    for t in range(2):
        wrap_rows(flat_rows, t * CART, rows_w, t)
    nothing = jnp.zeros((8, LANES), f32)
    for t in range(2):
        for d in separations:
            at = rows_of(d)
            spans = spans_of(rows_w, (t,), d)
            inverse = lax.rsqrt(spans[0] * spans[0] + spans[1] * spans[1] + spans[2] * spans[2])
            x = scale_ref[at, :] * inverse
            row_x[t, at, :] = x
        row_x[t, PAIRS:ROWS, :] = nothing
        sq = 0.0
        for start in range(0, ROWS, LANES):
            stop = min(start + LANES, ROWS)
            turned = row_x[t, start:stop, :].T
            high = turned.astype(bf16)
            rest = turned - high.astype(f32)
            at = slice(t * LANES, (t + 1) * LANES)
            rowx_hi[at, start:stop] = high
            rowx_lo[at, start:stop] = rest.astype(bf16)
            sq = sq + jnp.sum(turned * turned, axis=1, keepdims=True)
        row_sq[t * LANES : (t + 1) * LANES, :] = jnp.broadcast_to(sq, (LANES, LANES))


def apply_kernel(
    place, cols_ref, scale_ref, rows_w, rowx_hi, rowx_lo, row_sq, out_ref,
    flat_cols, cols_p, cols_c, pair_hi, pair_lo, col_x, col_weight, grads, back, flat_out,
):
    flat_cols[...] = cols_ref[...].T
    for t in range(2):
        wrap_rows(flat_cols, t * CART, cols_p, t)
        wrap_rows(flat_cols, (2 + t) * CART, cols_c, t)

    extra = jnp.where(lax.broadcasted_iota(jnp.int32, (8, LANES), 0) == 0, 1.0, 0.0)
    nothing = jnp.zeros((8, LANES), f32)
    col_sq, col_xu = [], []
    for t in range(2):
        sq = nothing
        lanes_x = slice(t * LANES, (t + 1) * LANES)
        for d in separations:
            spans = spans_of(cols_p, (t,), d)
            inverse = lax.rsqrt(spans[0] * spans[0] + spans[1] * spans[1] + spans[2] * spans[2])
            at = rows_of(d)
            x = scale_ref[at, :] * inverse
            sq = sq + fold8(x * x)
            col_x[t, at, :] = x
            col_weight[t, at, :] = x * inverse * inverse
            if d == 0:
                x = jnp.concatenate([x, extra], 0)
                at = slice(LAST, ROWS)
            pair_hi[at, lanes_x], pair_lo[at, lanes_x] = halves(x)
        col_sq.append(jnp.sum(sq, axis=0, keepdims=True))

    count = 2 * LANES
    turned = jnp.concatenate([rowx_hi[...], rowx_lo[...]], axis=0)
    with_high, with_low = dot_nn(turned, pair_hi[:, :count]), dot_nn(turned, pair_lo[:, :count])
    gram = (with_high[:count] + with_high[count:]) + (with_low[:count] + with_low[count:])

    for t in range(2):
        xu = nothing
        lanes_u = slice((2 + t) * LANES, (3 + t) * LANES)
        for d in separations:
            spans = spans_of(cols_p, (t,), d)
            moves = spans_of(cols_c, (t,), d)
            at = rows_of(d)
            along = spans[0] * moves[0] + spans[1] * moves[1] + spans[2] * moves[2]
            u = -col_weight[t, at, :] * along
            xu = xu + fold8(col_x[t, at, :] * u)
            if d == 0:
                u = jnp.concatenate([u, nothing], 0)
                at = slice(LAST, ROWS)
            pair_hi[at, lanes_u], pair_lo[at, lanes_u] = halves(u)
        col_xu.append(jnp.sum(xu, axis=0, keepdims=True))

    with_high = dot_nn(turned, pair_hi[:, count:])
    cross = with_high[:count] + with_high[count:] + dot_nn(rowx_hi[...], pair_lo[:, count:])
    sq_dist = row_sq[:, 0:1] + jnp.concatenate(col_sq, axis=1) - 2.0 * gram
    radius = jnp.sqrt(jnp.maximum(sq_dist, 0.0))
    envelope = outer_factor * jnp.exp(-decay_rate * radius)
    direct = envelope * (1.0 + decay_rate * radius)
    bent = (radial_factor * envelope) * (cross - jnp.concatenate(col_xu, axis=1))
    high, low = halves(jnp.concatenate([bent, direct], axis=1))
    for t in range(2):
        back[t] = jnp.zeros(back.shape[1:], f32)

    def multiply(first, end):
        at = slice((first - 1) * GROUP, ROWS if end == 9 else (end - 1) * GROUP)
        part_hi, part_lo = pair_hi[at, :], pair_lo[at, :]
        both = dot_nt(jnp.concatenate([part_hi, part_lo], axis=0), high)
        size = part_hi.shape[0]
        grads[at, :] = both[:size] + both[size:] + dot_nt(part_hi, low)

    def terms_of(t, d):
        at, lanes = rows_of(d), slice(t * LANES, (t + 1) * LANES)
        spans = spans_of(rows_w, (t,), d)
        inverse = lax.rsqrt(spans[0] * spans[0] + spans[1] * spans[1] + spans[2] * spans[2])
        x = scale_ref[at, :] * inverse
        bend = grads[PAIRS : PAIRS + 1, lanes]
        pull = (x * inverse * inverse) * (grads[at, lanes] - bend * x)
        return [pull * span for span in spans]

    def pull_back(t, first, end):
        here = [jnp.zeros((BLOCK, LANES), f32) for _ in range(3)]
        if end == 9:
            for k, term in enumerate(terms_of(t, 0)):
                back[t, k, 0:HALF, :] = term
                back[t, k, ATOMS - 1 : ATOMS, :] = -jnp.sum(term, axis=0, keepdims=True)
        for shift in range(first, end):
            there = [None] * 3
            for step in range(3):
                for k, term in enumerate(terms_of(t, shift + 8 * step)):
                    here[k] = here[k] + term
                    pieces = [term[8 * n : 8 * n + 8] for n in range(BLOCK // 8)]
                    if step == 0:
                        there[k] = pieces
                        continue
                    for n, piece in enumerate(pieces):
                        if step + n < len(there[k]):
                            there[k][step + n] = there[k][step + n] + piece
                        else:
                            there[k].append(piece)
            for k in range(3):
                total = jnp.concatenate(there[k], axis=0)
                at = slice(shift, shift + total.shape[0])
                back[t, k, at, :] = back[t, k, at, :] + total
        for k in range(3):
            back[t, k, 0:BLOCK, :] = back[t, k, 0:BLOCK, :] - here[k]

    multiply(*PARTS[0])
    for n, part in enumerate(PARTS):
        if n + 1 < len(PARTS):
            multiply(*PARTS[n + 1])
        for t in range(2):
            pull_back(t, *part)
    for t in range(2):
        for k in range(3):
            back[t, k, 0 : WRAP - ATOMS, :] = back[t, k, 0 : WRAP - ATOMS, :] + back[t, k, ATOMS:WRAP, :]
            base = t * CART + k * ATOMS
            flat_out[base : base + ATOMS, :] = back[t, k, 0:ATOMS, :]
    turned = flat_out[...].T
    for n, (at, size) in enumerate(place(flat_out.shape[1] // HALF_ROWS)):
        out_ref[pl.ds(at, size), :] = turned[n * size : (n + 1) * size, :]


def vmem(count):
    return [pl.BlockSpec(memory_space=pltpu.VMEM)] * count


def shape(*dims, kind=f32):
    return jax.ShapeDtypeStruct(dims, kind)


params = pltpu.CompilerParams(vmem_limit_bytes=16 * 1024 * 1024)


def scale_table(atom_pairs, pair_scale):
    return pl.pallas_call(
        spread_scale,
        out_shape=shape(ROWS, LANES),
        in_specs=vmem(2),
        out_specs=vmem(1)[0],
        compiler_params=params,
        cost_estimate=pl.CostEstimate(
            flops=20_000_000, bytes_accessed=700_000, transcendentals=0
        ),
    )(atom_pairs, pair_scale.reshape(1, -1))


def row_terms(rows, atom_pairs, pair_scale):
    scale = scale_table(atom_pairs, pair_scale)
    terms = pl.pallas_call(
        rows_kernel,
        out_shape=(
            shape(2, 3, WRAP, LANES),
            shape(2 * LANES, KDIM, kind=bf16),
            shape(2 * LANES, KDIM, kind=bf16),
            shape(2 * LANES, LANES),
        ),
        in_specs=vmem(2),
        out_specs=tuple(vmem(4)),
        scratch_shapes=[pltpu.VMEM((2 * CART, LANES), f32), pltpu.VMEM((2, ROWS, LANES), f32)],
        compiler_params=params,
        cost_estimate=pl.CostEstimate(
            flops=40_000_000, bytes_accessed=6_000_000, transcendentals=300_000
        ),
    )(rows, scale)
    return scale, *terms


def cols_apply(cols, terms, place):
    return pl.pallas_call(
        functools.partial(apply_kernel, place),
        out_shape=shape(LANES, 2 * CART),
        in_specs=vmem(1 + len(terms)),
        out_specs=vmem(1)[0],
        scratch_shapes=[
            pltpu.VMEM((4 * CART, LANES), f32),
            pltpu.VMEM((2, 3, WRAP, LANES), f32),
            pltpu.VMEM((2, 3, WRAP, LANES), f32),
            pltpu.VMEM((KDIM, 4 * LANES), bf16),
            pltpu.VMEM((KDIM, 4 * LANES), bf16),
            pltpu.VMEM((2, ROWS, LANES), f32),
            pltpu.VMEM((2, ROWS, LANES), f32),
            pltpu.VMEM((ROWS, 2 * LANES), f32),
            pltpu.VMEM((2, 3, WRAP, LANES), f32),
            pltpu.VMEM((2 * CART, LANES), f32),
        ],
        compiler_params=params,
        cost_estimate=pl.CostEstimate(
            flops=2_000_000_000, bytes_accessed=6_000_000, transcendentals=500_000
        ),
    )(cols, *terms)


def as_they_are(count):
    return [(0, count * HALF_ROWS)]


def tile_apply(rows, cols, atom_pairs, pair_scale, place=as_they_are):
    return cols_apply(cols, row_terms(rows, atom_pairs, pair_scale), place)


def side_by_side(value):
    half = value.shape[0] // 2
    return jnp.concatenate([value[:half], value[half:]], axis=1)


def exchange(value, axis):
    return lax.all_to_all(value, axis, split_axis=0, concat_axis=0, tiled=True)


def from_everyone(value, axis):
    copies = jnp.broadcast_to(value, (lax.axis_size(axis), *value.shape))
    return exchange(copies, axis).reshape(-1, value.shape[1])


def in_groups(value, axis, size):
    groups = [list(range(n, n + size)) for n in range(0, lax.axis_size(axis), size)]
    return lax.all_gather(value, axis, axis=0, tiled=True, axis_index_groups=groups)


def with_partners(value, axis, steps):
    count = lax.axis_size(axis)
    moved = [lax.ppermute(value, axis, [(n, n ^ step) for n in range(count)]) for step in steps]
    return jnp.concatenate([value, *moved], axis=0)


def row_gather(value, axis):
    return in_groups(with_partners(value, axis, (4, 8, 12)), axis, 4)


def owners_place(count):
    own = lax.axis_index("row")
    first = 4 * (own // 4)
    numbers = [(first ^ step) + n for n in range(4) for step in (0, 4, 8, 12)]
    return [(pl.multiple_of(at * HALF_ROWS, HALF_ROWS), HALF_ROWS) for at in numbers]


def on_device(positions, coefficients, atom_pairs, pair_scale):
    packed = jnp.concatenate([side_by_side(positions), side_by_side(coefficients)], axis=1)
    cols = from_everyone(packed, "col")
    rows = row_gather(packed[:, : 2 * CART], "row")
    partial = tile_apply(rows, cols, atom_pairs, pair_scale, owners_place)
    arrived = exchange(partial.reshape(lax.axis_size("row"), -1, 2 * CART), "row")
    total = arrived.sum(axis=0)
    return jnp.concatenate([total[:, :CART], total[:, CART:]], axis=0)


def solution(mesh):
    in_specs = (P(("row", "col"), None), P(("row", "col"), None), P(), P())
    out_specs = P(("row", "col"), None)
    return jax.shard_map(
        on_device, mesh=mesh, in_specs=in_specs, out_specs=out_specs, check_vma=False
    )
```
